32 devices in a mesh: space: 8 (over y, x, core), load: 4 (over z).
Axes of the slice: x: 2, y: 2, z: 4, core: 2. Of those that a mesh axis runs over, the one named last changes fastest.
Arguments:
- load_force: float32 [4, 3, 64, 16, 256], P('load', None, 'space'), may hold values from -6 to 6
- stiffness: float32 [64, 16, 256], P('space'), may hold values from 0.5 to 4
- material: int32 [8, 2], P('space'), may hold values from 0 to 2
- face_src: int32 [8, 8, 256], P('space'), may hold values from 0 to 32767
- face_count: int32 [8, 8], P('space'), may hold values from 0 to 256, as said below
- face_dst: int32 [8, 8, 256], P('space'), may hold values from 0 to 4095
Outputs:
- displacement: float32 [4, 3, 64, 16, 256], P('load', None, 'space')
- sensitivity: float32 [3, 64, 16, 256], P(None, 'space', 'load')
The draws below stay inside these ranges and needn't reach their ends.
Inputs may be any that keep to these rules, and one draw needn't show every extreme that they name: face_count[s, o] counts the live first slots from slab s to owner o; in every row one owner gets all 256.
All inputs are finite; a program needn't handle non-finite values.
Results may differ from the reference program's by a relative error of at most 0.0001.
Values sent between devices are 32-bit elements; how exact they have to be, the bound alone decides.
A program may use at most 192 MiB of HBM per device.

```python
import math
import jax
import jax.numpy as jnp

CX = 8
NY = 16
NZ = 256
BY = 8
SLOTS = 256
FINE_STEPS = 3
COARSE_STEPS = 4
NX = 64
OWNERS = 8
LOADS = 4


def draw_face_count(key, part):
    key_quiet, key_busy, key_hot = jax.random.split(key, 3)
    quiet_load = jax.random.randint(key_quiet, (OWNERS, OWNERS), 0, SLOTS // 2 + 1)
    busy_load = jax.random.randint(key_busy, (OWNERS, OWNERS), SLOTS // 2, SLOTS + 1)
    hot_owner = jax.random.randint(key_hot, (1, OWNERS), 0, 8) == 0
    counts = jnp.where(hot_owner, busy_load, quiet_load)
    row_ids = jnp.arange(OWNERS, dtype=jnp.int32)[:, None]
    col_ids = jnp.arange(OWNERS, dtype=jnp.int32)[None, :]
    return jnp.where(col_ids == (row_ids + 1) % OWNERS, SLOTS, counts).astype(jnp.int32)


def place_ends(drawn, rng, smallest, high):
    extent = drawn.shape
    spot = [jax.random.randint(jax.random.fold_in(rng, axis), (), 0, extent[axis]) for axis in range(len(extent))]
    drawn = drawn.at[tuple(spot)].set(smallest)
    longest = extent.index(max(extent))
    spot[longest] = (spot[longest] + 1) % extent[longest]
    return drawn.at[tuple(spot)].set(high)


def steps_of(own_key, shape, cuts, least, high):
    level, own = 1.0, jax.random.fold_in(own_key, 6)
    for position, shards_of in cuts:
        steps = jnp.exp(jax.random.uniform(jax.random.fold_in(own, position), (shards_of,), jnp.float32, least / len(cuts), high / len(cuts)))
        level = level * jnp.repeat(steps, shape[position] // shards_of).reshape([-1 if axis == position else 1 for axis in range(len(shape))])
    return level


def bell_draw(rng, dims, scale, reach, cuts=(), kind=jnp.bfloat16):
    factor_of = steps_of(rng, dims, cuts, -0.22, 0.18) if cuts else 1.0
    values = jax.random.normal(rng, dims, jnp.float32) * scale * factor_of
    return jnp.minimum(jnp.maximum(values, -reach), reach).astype(kind)


def setup_inputs(seed: int = 0) -> dict:
    key_list = jax.random.split(jax.random.key(seed), 7)
    return {
        "load_force": bell_draw(key_list[0], (LOADS, 3, NX, NY, NZ), 1.0, 6.0, ((0, 4), (2, 8)), jnp.float32),
        "stiffness": jnp.clip(jnp.exp(math.log(4.0) - 2.0794415 * jax.random.uniform(key_list[1], (NX, NY, NZ), jnp.float32) ** steps_of(key_list[1], (NX, NY, NZ), ((0, 8),), -0.2, 0.2)), 0.5, 4.0),
        "material": place_ends(jax.random.randint(key_list[2], (OWNERS, NY // BY), 0, 3), jax.random.fold_in(key_list[2], 1), 0, 2).astype(jnp.int32),
        "face_src": place_ends(jax.random.randint(key_list[3], (OWNERS, OWNERS, SLOTS), 0, CX * NY * NZ), jax.random.fold_in(key_list[3], 1), 0, (CX * NY * NZ) - 1).astype(jnp.int32),
        "face_count": draw_face_count(jax.random.fold_in(key_list[6], 71), 0),
        "face_dst": place_ends(jax.random.randint(key_list[5], (OWNERS, OWNERS, SLOTS), 0, (CX // 2) * (NY // 2) * (NZ // 2)), jax.random.fold_in(key_list[5], 1), 0, ((CX // 2) * (NY // 2) * (NZ // 2)) - 1).astype(jnp.int32),
    }


UPPER_EDGE = 2.1
LOWER_EDGE = 0.15
COUPLING = 0.1
MODULI = (1.0, 0.55, 0.25)


def neighbour_list():
    entries = []
    for shift_x in (-1, 0, 1):
        for shift_y in (-1, 0, 1):
            for shift_z in (-1, 0, 1):
                reach_len = abs(shift_x) + abs(shift_y) + abs(shift_z)
                if reach_len > 0:
                    entries.append((shift_x, shift_y, shift_z, (1.0, 0.5, 0.25)[reach_len - 1] / 14.0))
    return entries


def window(padded, shift_x, shift_y, shift_z, inner_shape):
    size_x, size_y, size_z = inner_shape
    return padded[:, 1 + shift_x:1 + shift_x + size_x, 1 + shift_y:1 + shift_y + size_y, 1 + shift_z:1 + shift_z + size_z]


def operate(padded_field, padded_coef):
    inner_shape = (padded_field.shape[1] - 2, padded_field.shape[2] - 2, padded_field.shape[3] - 2)
    centre = window(padded_field, 0, 0, 0, inner_shape)
    coef_mid = window(padded_coef, 0, 0, 0, inner_shape)
    result = jnp.zeros_like(centre)
    for shift_x, shift_y, shift_z, weight in neighbour_list():
        face_coef = 0.5 * (coef_mid + window(padded_coef, shift_x, shift_y, shift_z, inner_shape))
        result = result + (weight * face_coef) * (centre - window(padded_field, shift_x, shift_y, shift_z, inner_shape))
    pieces = []
    for component in range(3):
        mixed_term = jnp.zeros_like(coef_mid[0])
        for partner in range(3):
            if partner != component:
                for sign_a in (1, -1):
                    for sign_b in (1, -1):
                        offset = [0, 0, 0]
                        offset[component] += sign_a
                        offset[partner] += sign_b
                        mixed_term = mixed_term + (0.25 * sign_a * sign_b) * window(padded_field[partner:partner + 1], offset[0], offset[1], offset[2], inner_shape)[0]
        pieces.append(result[component] - COUPLING * coef_mid[0] * mixed_term)
    return jnp.stack(pieces)


def diagonal_of(padded_coef):
    inner_shape = (padded_coef.shape[1] - 2, padded_coef.shape[2] - 2, padded_coef.shape[3] - 2)
    coef_mid = window(padded_coef, 0, 0, 0, inner_shape)
    total_sum = jnp.zeros_like(coef_mid)
    for shift_x, shift_y, shift_z, weight in neighbour_list():
        total_sum = total_sum + weight * 0.5 * (coef_mid + window(padded_coef, shift_x, shift_y, shift_z, inner_shape))
    return total_sum


def pad_global(grid_field):
    return jnp.pad(grid_field, ((0, 0), (1, 1), (1, 1), (1, 1)))


def chebyshev(source, padded_coef, diagonal, sweep_count, widen):
    midpoint = (UPPER_EDGE + LOWER_EDGE) / 2.0
    halfwidth = (UPPER_EDGE - LOWER_EDGE) / 2.0
    spread_ratio = midpoint / halfwidth
    rho_old = 1.0 / spread_ratio
    update = source / (midpoint * diagonal)
    solution = update
    for sweep_idx in range(1, sweep_count):
        residual = source - operate(widen(solution), padded_coef)
        rho_new = 1.0 / (2.0 * spread_ratio - rho_old)
        update = (rho_new * rho_old) * update + (2.0 * rho_new / halfwidth) * residual / diagonal
        solution = solution + update
        rho_old = rho_new
    return solution


def coarsen(grid_field):
    comps, size_x, size_y, size_z = grid_field.shape
    return grid_field.reshape(comps, size_x // 2, 2, size_y // 2, 2, size_z // 2, 2).mean(axis=(2, 4, 6))


def refine(grid_field):
    return jnp.repeat(jnp.repeat(jnp.repeat(grid_field, 2, axis=1), 2, axis=2), 2, axis=3)


def modulus_rows(material, brick_rows):
    onehot = (material[..., None] == jnp.arange(len(MODULI), dtype=jnp.int32)).astype(jnp.float32)
    values = jnp.sum(onehot * jnp.array(MODULI, jnp.float32), axis=-1)
    return jnp.repeat(values, brick_rows, axis=-1)


def reference(load_force, stiffness, material, face_src, face_count, face_dst):
    owners = NX // CX
    fine_cells = CX * NY * NZ
    coarse_cells = (CX // 2) * (NY // 2) * (NZ // 2)
    own_cells = jnp.repeat(modulus_rows(material, BY), CX, axis=0)[:, :, None]
    coef = stiffness * own_cells
    padded_coef = pad_global(coef[None])
    diag_fine = diagonal_of(padded_coef)
    padded_coarse = pad_global(coarsen(coef[None]))
    diag_coarse = diagonal_of(padded_coarse)
    sender = jnp.broadcast_to(jnp.arange(owners, dtype=jnp.int32)[:, None, None], face_src.shape)
    owner_idx = jnp.broadcast_to(jnp.arange(owners, dtype=jnp.int32)[None, :, None], face_src.shape)
    live_mask = (jnp.arange(SLOTS, dtype=jnp.int32)[None, None, :] < face_count[:, :, None]).astype(jnp.float32)
    targets = jnp.transpose(face_dst, (1, 0, 2))
    energy = jnp.zeros((NX, NY, NZ), jnp.float32)
    outputs = []
    for load_idx in range(LOADS):
        source = load_force[load_idx]
        smooth = chebyshev(source, padded_coef, diag_fine, FINE_STEPS, pad_global)
        residual = source - operate(pad_global(smooth), padded_coef)
        coarse_source = 4.0 * coarsen(residual)
        coarse_shape = coarse_source.shape
        picked = residual.reshape(3, owners, fine_cells)[:, sender, face_src] * live_mask
        coarse_source = coarse_source.reshape(3, owners, coarse_cells).at[:, owner_idx, targets].add(picked).reshape(coarse_shape)
        correction = chebyshev(coarse_source, padded_coarse, diag_coarse, COARSE_STEPS, pad_global)
        displaced = smooth + refine(correction)
        image = operate(pad_global(displaced), padded_coef)
        energy = energy + jnp.sum(displaced * image, axis=0)
        outputs.append(displaced)
    moduli = jnp.array(MODULI, jnp.float32)[:, None, None, None]
    sensitivity = (moduli - own_cells[None]) / own_cells[None] * energy[None]
    return jnp.stack(outputs), sensitivity
```

```python
import functools

import jax
import jax.numpy as jnp
from jax import lax
from jax.experimental import pallas as pl
from jax.experimental.pallas import tpu as pltpu
from jax.sharding import PartitionSpec as P

BY = 8
FINE_STEPS = 3
COARSE_STEPS = 4
UPPER_EDGE = 2.1
LOWER_EDGE = 0.15
COUPLING = 0.1
MODULI = (1.0, 0.55, 0.25)

MID = (UPPER_EDGE + LOWER_EDGE) / 2.0
HALF = (UPPER_EDGE - LOWER_EDGE) / 2.0
F32 = jnp.float32
BF16 = jnp.bfloat16
MESH = pl.DeviceIdType.MESH
FH = 4
CH = 4


def cheb_factors(count):
    spread = MID / HALF
    rho = 1.0 / spread
    out = []
    for _ in range(1, count):
        rho_new = 1.0 / (2.0 * spread - rho)
        out.append((rho_new * rho, 2.0 * rho_new / HALF))
        rho = rho_new
    return out


def split(x):
    hi = x.astype(BF16)
    return hi, (x - hi.astype(F32)).astype(BF16)


def dot2(x, table):
    hi, lo = split(x)
    return jnp.dot(hi, table, preferred_element_type=F32) + jnp.dot(
        lo, table, preferred_element_type=F32
    )


class Plane:
    def __init__(self, rows, lanes):
        self.rows, self.lanes = rows, lanes
        row = lax.broadcasted_iota(jnp.int32, (rows, lanes), 0)
        lane = lax.broadcasted_iota(jnp.int32, (rows, lanes), 1)
        self.masks = (row == rows - 1, row == 0, lane == lanes - 1, lane == 0)

    def yp(self, a):
        return jnp.where(self.masks[0], 0.0, pltpu.roll(a, self.rows - 1, 0))

    def ym(self, a):
        return jnp.where(self.masks[1], 0.0, pltpu.roll(a, 1, 0))

    def zp(self, a):
        return jnp.where(self.masks[2], 0.0, pltpu.roll(a, self.lanes - 1, 1))

    def zm(self, a):
        return jnp.where(self.masks[3], 0.0, pltpu.roll(a, 1, 1))

    def ty(self, a):
        return a + 0.5 * (self.yp(a) + self.ym(a))

    def tz(self, a):
        return a + 0.5 * (self.zp(a) + self.zm(a))

    def apply(self, v, w, coef, p):
        u0 = [v[c, p] for c in range(3)]
        um = [v[c, p - 1] for c in range(3)]
        up = [v[c, p + 1] for c in range(3)]
        a = [(u0[c] + 0.5 * (um[c] + up[c])) * (1.0 / 14.0) for c in range(3)]
        e = [(up[c] - um[c]) * (0.5 * COUPLING) for c in range(3)]
        b = [(w[c, p] + 0.5 * (w[c, p - 1] + w[c, p + 1])) * (1.0 / 14.0) for c in range(3)]
        half = 0.5 * COUPLING
        t = self.ty(a[0])
        mix_x = (
            t
            + 0.5 * (self.zp(t + e[2]) + self.zm(t - e[2]))
            + 0.5 * (self.yp(e[1]) - self.ym(e[1]))
        )
        t = self.tz(a[1])
        g = e[0] + half * (self.zp(u0[2]) - self.zm(u0[2]))
        mix_y = t + 0.5 * (self.yp(t + g) + self.ym(t - g))
        t = self.ty(a[2])
        g = e[0] + half * (self.yp(u0[1]) - self.ym(u0[1]))
        mix_z = t + 0.5 * (self.zp(t + g) + self.zm(t - g))
        k, dk = coef[0, p], coef[1, p]
        mix = (mix_x, mix_y, mix_z)
        return [dk * u0[c] - k * mix[c] - self.tz(self.ty(b[c])) for c in range(3)]

    def diag(self, k, p):
        t = k[p] + 0.5 * (k[p - 1] + k[p + 1])
        return (3.0 / 7.0) * k[p] + self.tz(self.ty(t)) * (1.0 / 14.0)


def planes_loop(low, high, unroll, step):
    def run(p, carry):
        step(p)
        return carry

    lax.fori_loop(low, high, run, 0, unroll=unroll)


def start_sweep(low, high, unroll, src, coef, d, v, w):
    def step(p):
        scale = coef[2, p] * (1.0 / MID)
        k = coef[0, p]
        for c in range(3):
            new = src[c, p] * scale
            d[c, p] = new
            v[c, p] = new
            w[c, p] = k * new

    planes_loop(low, high, unroll, step)


def sweep(plane, low, high, unroll, factors, src, coef, d, v, w, v_out, w_out):
    alpha, beta = factors

    def step(p):
        image = plane.apply(v, w, coef, p)
        k = coef[0, p]
        scale = coef[2, p] * beta
        for c in range(3):
            new = alpha * d[c, p] + scale * (src[c, p] - image[c])
            d[c, p] = new
            total = v[c, p] + new
            v_out[c, p] = total
            w_out[c, p] = k * total

    planes_loop(low, high, unroll, step)


def kernel(
    n, loads,
    force, stiff, mat, face_src, count, face_dst,
    disp_out, sens_out,
    src, raw, coef, d, va, wa, vb, wb, res, pooled, kc, ccoef, csrc, cd, cva, cwa, cvb, cwb,
    wide, sendbuf, arrived, esend, erecv,
    local_sem, send_sem, recv_sem, a_send, a_recv, e_send, e_recv,
):
    me = lax.axis_index("space")
    load = lax.axis_index("load")
    cx, ny, nz = raw.shape
    hx, hy, hz = cx // 2, ny // 2, nz // 2
    fine = Plane(ny, nz)
    coarse = Plane(hy, hz)
    slots = face_src.shape[2]
    top = cx + 2 * FH
    ctop = hx + 2 * CH

    barrier = pltpu.get_barrier_semaphore()

    @pl.loop(1, n)
    def _(k):
        pl.semaphore_signal(
            barrier, inc=1, device_id={"space": lax.rem(me + k, n)}, device_id_type=MESH
        )

    @pl.loop(1, loads)
    def _(k):
        pl.semaphore_signal(
            barrier, inc=1, device_id={"load": lax.rem(load + k, loads)}, device_id_type=MESH
        )

    get_stiff = pltpu.make_async_copy(stiff, raw, local_sem.at[0])
    get_force = pltpu.make_async_copy(force.at[0], src.at[:, pl.ds(FH, cx)], local_sem.at[1])
    get_stiff.start()
    get_force.start()

    right = lax.rem(me + 1, n)
    left = lax.rem(me + n - 1, n)

    def pair(kind, to_right, to_left):
        made = []
        for side, (ends, target) in enumerate(((to_right, right), (to_left, left))):
            made.append(
                pltpu.make_async_remote_copy(
                    src_ref=ends[0], dst_ref=ends[1],
                    send_sem=send_sem.at[kind, side], recv_sem=recv_sem.at[kind, side],
                    device_id={"space": target}, device_id_type=MESH,
                )
            )
        return made

    fw = FH - 1
    force_pair = pair(
        0,
        (force.at[0, :, pl.ds(cx - fw, fw)], src.at[:, pl.ds(1, fw)]),
        (force.at[0, :, pl.ds(0, fw)], src.at[:, pl.ds(FH + cx, fw)]),
    )
    coef_pair = pair(
        1,
        (coef.at[0, pl.ds(cx, FH)], coef.at[0, pl.ds(0, FH)]),
        (coef.at[0, pl.ds(FH, FH)], coef.at[0, pl.ds(FH + cx, FH)]),
    )
    ccoef_pair = pair(
        2,
        (ccoef.at[:, pl.ds(CH, hx)], ccoef.at[:, pl.ds(0, hx)]),
        (ccoef.at[:, pl.ds(CH, hx)], ccoef.at[:, pl.ds(CH + hx, hx)]),
    )
    csrc_pair = pair(
        3,
        (csrc.at[:, pl.ds(CH, hx)], csrc.at[:, pl.ds(0, hx)]),
        (csrc.at[:, pl.ds(CH, hx)], csrc.at[:, pl.ds(CH + hx, hx)]),
    )
    has_left, has_right = me > 0, me < n - 1

    def start(made):
        @pl.when(has_right)
        def _():
            made[0].start()

        @pl.when(has_left)
        def _():
            made[1].start()

    def land(made):
        @pl.when(has_left)
        def _():
            made[0].wait_recv()

        @pl.when(has_right)
        def _():
            made[1].wait_recv()

    def sent(made):
        @pl.when(has_right)
        def _():
            made[0].wait_send()

        @pl.when(has_left)
        def _():
            made[1].wait_send()

    @pl.when(me == 0)
    def _():
        src[:, 0:FH] = jnp.zeros((3, FH, ny, nz), F32)
        coef[0, 0:FH] = jnp.zeros((FH, ny, nz), F32)
        ccoef[:, 0:CH] = jnp.zeros((3, CH, hy, hz), F32)
        csrc[:, 0:CH] = jnp.zeros((3, CH, hy, hz), F32)

    @pl.when(me == n - 1)
    def _():
        src[:, FH + cx : top] = jnp.zeros((3, FH, ny, nz), F32)
        coef[0, FH + cx : top] = jnp.zeros((FH, ny, nz), F32)
        ccoef[:, CH + hx : ctop] = jnp.zeros((3, CH, hy, hz), F32)
        csrc[:, CH + hx : ctop] = jnp.zeros((3, CH, hy, hz), F32)

    def by_material(brick, values):
        m = mat[0, brick]
        return jnp.where(m == 0, values[0], jnp.where(m == 1, values[1], values[2]))

    get_stiff.wait()
    for brick in range(ny // BY):
        own = by_material(brick, MODULI)
        rows = slice(brick * BY, (brick + 1) * BY)
        coef[0, FH : FH + cx, rows] = raw[:, rows] * own

    pl.semaphore_wait(barrier, n - 1 + loads - 1)
    start(coef_pair)
    start(force_pair)

    pool = (
        lax.shift_right_logical(lax.broadcasted_iota(jnp.int32, (nz, hz), 0), 1)
        == lax.broadcasted_iota(jnp.int32, (nz, hz), 1)
    ).astype(F32).astype(BF16)
    spread = (
        lax.shift_right_logical(lax.broadcasted_iota(jnp.int32, (hz, nz), 1), 1)
        == lax.broadcasted_iota(jnp.int32, (hz, nz), 0)
    ).astype(F32).astype(BF16)

    def pool_rows(i):
        return pooled[i, pl.ds(0, hy, stride=2), :] + pooled[i, pl.ds(1, hy, stride=2), :]

    land(coef_pair)
    kview = coef.at[0]

    def diag_step(p):
        diag = fine.diag(kview, p)
        inside = jnp.logical_and(
            jnp.logical_or(p >= FH, has_left), jnp.logical_or(p < FH + cx, has_right)
        )
        keep = jnp.where(inside, 1.0, 0.0)
        coef[1, p] = diag + coef[0, p] * (1.0 / 7.0)
        coef[2, p] = keep / jnp.where(inside, diag, 1.0)

    planes_loop(1, top - 1, 1, diag_step)

    count_c = hx + 2
    first = FH - 2
    stack = jnp.concatenate(
        [coef[0, first + 2 * i] + coef[0, first + 2 * i + 1] for i in range(count_c)], axis=0
    )
    pooled[0:count_c] = dot2(stack, pool).reshape(count_c, ny, hz)
    for i in range(count_c):
        kc[i] = pool_rows(i) * 0.125
    for i in range(hx):
        diag = coarse.diag(kc, i + 1)
        ccoef[0, CH + i] = kc[i + 1]
        ccoef[1, CH + i] = diag + kc[i + 1] * (1.0 / 7.0)
        ccoef[2, CH + i] = 1.0 / diag
    start(ccoef_pair)

    get_force.wait()
    land(force_pair)

    factors = cheb_factors(FINE_STEPS)
    start_sweep(1, top - 1, 2, src, coef, d, va, wa)
    sweep(fine, 2, top - 2, 1, factors[0], src, coef, d, va, wa, vb, wb)
    sweep(fine, 3, top - 3, 1, factors[1], src, coef, d, vb, wb, va, wa)

    def residual_step(p):
        image = fine.apply(va, wa, coef, p)
        for c in range(3):
            res[c, p - FH] = src[c, p] - image[c]

    planes_loop(FH, FH + cx, 1, residual_step)

    rows_f = cx * ny
    flat = res[...].reshape(3 * rows_f, nz)
    flat_hi, flat_lo = split(flat)
    wide[0] = flat_hi
    wide[1] = flat_lo
    zbits = nz.bit_length() - 1
    hbits = hz.bit_length() - 1
    sub_z = lax.broadcasted_iota(jnp.int32, (nz, slots), 0)
    sub_r = lax.broadcasted_iota(jnp.int32, (rows_f, slots), 0)
    slot_r = lax.broadcasted_iota(jnp.int32, (rows_f, slots), 1)

    def pick(owner):
        index = face_src[0, pl.ds(owner, 1), :]
        lanes = (sub_z == jnp.bitwise_and(index, nz - 1)).astype(F32).astype(BF16)
        found = jnp.dot(wide[0], lanes, preferred_element_type=F32) + jnp.dot(
            wide[1], lanes, preferred_element_type=F32
        )
        live = jnp.logical_and(
            sub_r == lax.shift_right_logical(index, zbits), slot_r < count[0, owner]
        )
        return [
            jnp.sum(
                jnp.where(live, found[c * rows_f : (c + 1) * rows_f], 0.0), axis=0, keepdims=True
            )
            for c in range(3)
        ]

    def a_copy(k):
        owner = lax.rem(me + k, n)
        return pltpu.make_async_remote_copy(
            src_ref=sendbuf.at[owner], dst_ref=arrived.at[me],
            send_sem=a_send.at[k], recv_sem=a_recv.at[k],
            device_id={"space": owner}, device_id_type=MESH,
        )

    zero_tail = jnp.zeros((5, slots), F32)

    @pl.loop(1, n)
    def _(k):
        owner = lax.rem(me + k, n)
        sendbuf[owner] = jnp.concatenate(pick(owner) + [zero_tail], axis=0)
        a_copy(k).start()

    arrived[me] = jnp.concatenate(pick(me) + [zero_tail], axis=0)

    for c in range(3):
        stack = jnp.concatenate([res[c, 2 * i] + res[c, 2 * i + 1] for i in range(hx)], axis=0)
        pooled[0:hx] = dot2(stack, pool).reshape(hx, ny, hz)
        for i in range(hx):
            csrc[c, CH + i] = pool_rows(i) * 0.5

    rows_c = hx * hy
    sub_l = lax.broadcasted_iota(jnp.int32, (hz, slots), 0)
    sub_c = lax.broadcasted_iota(jnp.int32, (rows_c, slots), 0)

    def place(sender):
        index = face_dst[0, pl.ds(sender, 1), :]
        lanes = (sub_l == jnp.bitwise_and(index, hz - 1)).astype(F32).astype(BF16)
        at_row = sub_c == lax.shift_right_logical(index, hbits)
        values = arrived[sender]
        parts = [jnp.where(at_row, values[c : c + 1], 0.0) for c in range(3)]
        hi, lo = split(jnp.concatenate(parts, axis=0))
        dims = (((1,), (1,)), ((), ()))
        return lax.dot_general(hi, lanes, dims, preferred_element_type=F32) + lax.dot_general(
            lo, lanes, dims, preferred_element_type=F32
        )

    def add_sender(k, total):
        a_copy(k).wait_recv()
        return total + place(lax.rem(me + n - k, n))

    total = lax.fori_loop(1, n, add_sender, place(me))
    csrc[:, CH : CH + hx] += total.reshape(3, hx, hy, hz)
    start(csrc_pair)
    land(ccoef_pair)
    land(csrc_pair)

    factors = cheb_factors(COARSE_STEPS)
    start_sweep(0, ctop, 2, csrc, ccoef, cd, cva, cwa)
    sweep(coarse, 1, ctop - 1, 2, factors[0], csrc, ccoef, cd, cva, cwa, cvb, cwb)
    sweep(coarse, 2, ctop - 2, 2, factors[1], csrc, ccoef, cd, cvb, cwb, cva, cwa)
    sweep(coarse, 3, ctop - 3, 2, factors[2], csrc, ccoef, cd, cva, cwa, cvb, cwb)

    fresh = hx + 2
    for c in range(3):
        lifted = dot2(cvb[c, 3 : 3 + fresh].reshape(fresh * hy, hz), spread)
        for i in range(fresh):
            plane = lifted[i * hy : (i + 1) * hy]
            doubled = jnp.broadcast_to(plane[:, None, :], (hy, 2, nz)).reshape(ny, nz)
            for p in (FH - 2 + 2 * i, FH - 1 + 2 * i):
                if FH - 1 <= p <= FH + cx:
                    vb[c, p] = va[c, p] + doubled
                    wb[c, p] = coef[0, p] * vb[c, p]

    put_disp = pltpu.make_async_copy(
        vb.at[:, pl.ds(FH, cx)], disp_out.at[0], local_sem.at[2]
    )
    put_disp.start()

    part = ny // loads

    def energy_step(p):
        image = fine.apply(vb, wb, coef, p)
        energy = vb[0, p] * image[0] + vb[1, p] * image[1] + vb[2, p] * image[2]
        for i in range(loads):
            esend[i, p - FH] = energy[i * part : (i + 1) * part]

    planes_loop(FH, FH + cx, 1, energy_step)

    def e_copy(k):
        owner = lax.rem(load + k, loads)
        return pltpu.make_async_remote_copy(
            src_ref=esend.at[owner], dst_ref=erecv.at[k],
            send_sem=e_send.at[k], recv_sem=e_recv.at[k],
            device_id={"load": owner}, device_id_type=MESH,
        )

    for k in range(1, loads):
        e_copy(k).start()

    sent(force_pair)
    sent(coef_pair)
    sent(ccoef_pair)
    sent(csrc_pair)

    @pl.loop(1, n)
    def _(k):
        a_copy(k).wait_send()

    total = esend[load]
    for k in range(1, loads):
        e_copy(k).wait_recv()
        total = total + erecv[k]
    brick = (load * part) // BY
    for m, modulus in enumerate(MODULI):
        ratio = by_material(brick, [(modulus - own) / own for own in MODULI])
        sens_out[m] = total * ratio
    for k in range(1, loads):
        e_copy(k).wait_send()
    put_disp.wait()


def body(n, loads, load_force, stiffness, material, face_src, face_count, face_dst):
    cx, ny, nz = stiffness.shape
    hx, hy, hz = cx // 2, ny // 2, nz // 2
    slots = face_src.shape[2]
    part = ny // loads
    fine = (cx + 2 * FH, ny, nz)
    coarse = (hx + 2 * CH, hy, hz)
    vmem = pl.BlockSpec(memory_space=pltpu.VMEM)
    smem = pl.BlockSpec(memory_space=pltpu.SMEM)
    hbm = pl.BlockSpec(memory_space=pl.ANY)

    def buf(*shape):
        return pltpu.VMEM(shape, F32)

    dma = pltpu.SemaphoreType.DMA
    return pl.pallas_call(
        functools.partial(kernel, n, loads),
        out_shape=(
            jax.ShapeDtypeStruct(load_force.shape, F32),
            jax.ShapeDtypeStruct((3, cx, part, nz), F32),
        ),
        in_specs=[hbm, hbm, smem, vmem, smem, vmem],
        out_specs=(hbm, vmem),
        scratch_shapes=[
            buf(3, *fine), buf(cx, ny, nz), buf(3, *fine), buf(3, *fine),
            buf(3, *fine), buf(3, *fine), buf(3, *fine), buf(3, *fine),
            buf(3, cx, ny, nz), buf(hx + 2, ny, hz), buf(hx + 2, hy, hz),
            buf(3, *coarse), buf(3, *coarse), buf(3, *coarse),
            buf(3, *coarse), buf(3, *coarse), buf(3, *coarse), buf(3, *coarse),
            pltpu.VMEM((2, 3 * cx * ny, nz), BF16),
            buf(n, 8, slots), buf(n, 8, slots),
            buf(loads, cx, part, nz), buf(loads, cx, part, nz),
            dma((3,)), dma((4, 2)), dma((4, 2)),
            dma((n,)), dma((n,)), dma((loads,)), dma((loads,)),
        ],
        compiler_params=pltpu.CompilerParams(
            collective_id=0, has_side_effects=True, vmem_limit_bytes=40 * 1024 * 1024
        ),
    )(load_force, stiffness, material, face_src, face_count, face_dst)


def solution(mesh):
    return jax.shard_map(
        functools.partial(body, mesh.shape["space"], mesh.shape["load"]),
        mesh=mesh,
        in_specs=(
            P("load", None, "space", None, None),
            P("space", None, None),
            P("space", None),
            P("space", None, None),
            P("space", None),
            P("space", None, None),
        ),
        out_specs=(P("load", None, "space", None, None), P(None, "space", "load", None)),
        check_vma=False,
    )
```

```python
import functools

import jax
import jax.numpy as jnp
from jax import lax
from jax.experimental import pallas as pl
from jax.experimental.pallas import tpu as pltpu
from jax.sharding import PartitionSpec as P

BY = 8
FINE_STEPS = 3
COARSE_STEPS = 4
UPPER_EDGE = 2.1
LOWER_EDGE = 0.15
COUPLING = 0.1
MODULI = (1.0, 0.55, 0.25)

MID = (UPPER_EDGE + LOWER_EDGE) / 2.0
HALF = (UPPER_EDGE - LOWER_EDGE) / 2.0
F32 = jnp.float32
BF16 = jnp.bfloat16
MESH = pl.DeviceIdType.MESH
FH = 4
CH = 4


def cheb_factors(count):
    spread = MID / HALF
    rho = 1.0 / spread
    out = []
    for _ in range(1, count):
        rho_new = 1.0 / (2.0 * spread - rho)
        out.append((rho_new * rho, 2.0 * rho_new / HALF))
        rho = rho_new
    return out


def split(x):
    hi = x.astype(BF16)
    return hi, (x - hi.astype(F32)).astype(BF16)


def dot2(x, table):
    hi, lo = split(x)
    return jnp.dot(hi, table, preferred_element_type=F32) + jnp.dot(
        lo, table, preferred_element_type=F32
    )


class Plane:
    def __init__(self, rows, lanes):
        self.rows, self.lanes = rows, lanes
        row = lax.broadcasted_iota(jnp.int32, (rows, lanes), 0)
        lane = lax.broadcasted_iota(jnp.int32, (rows, lanes), 1)
        self.masks = (row == rows - 1, row == 0, lane == lanes - 1, lane == 0)

    def yp(self, a):
        return jnp.where(self.masks[0], 0.0, pltpu.roll(a, self.rows - 1, 0))

    def ym(self, a):
        return jnp.where(self.masks[1], 0.0, pltpu.roll(a, 1, 0))

    def zp(self, a):
        return jnp.where(self.masks[2], 0.0, pltpu.roll(a, self.lanes - 1, 1))

    def zm(self, a):
        return jnp.where(self.masks[3], 0.0, pltpu.roll(a, 1, 1))

    def ty(self, a):
        return a + 0.5 * (self.yp(a) + self.ym(a))

    def tz(self, a):
        return a + 0.5 * (self.zp(a) + self.zm(a))

    def apply(self, v, w, coef, p):
        u0 = [v[c, p] for c in range(3)]
        um = [v[c, p - 1] for c in range(3)]
        up = [v[c, p + 1] for c in range(3)]
        a = [(u0[c] + 0.5 * (um[c] + up[c])) * (1.0 / 14.0) for c in range(3)]
        e = [(up[c] - um[c]) * (0.5 * COUPLING) for c in range(3)]
        b = [(w[c, p] + 0.5 * (w[c, p - 1] + w[c, p + 1])) * (1.0 / 14.0) for c in range(3)]
        half = 0.5 * COUPLING
        t = self.ty(a[0])
        mix_x = (
            t
            + 0.5 * (self.zp(t + e[2]) + self.zm(t - e[2]))
            + 0.5 * (self.yp(e[1]) - self.ym(e[1]))
        )
        t = self.tz(a[1])
        g = e[0] + half * (self.zp(u0[2]) - self.zm(u0[2]))
        mix_y = t + 0.5 * (self.yp(t + g) + self.ym(t - g))
        t = self.ty(a[2])
        g = e[0] + half * (self.yp(u0[1]) - self.ym(u0[1]))
        mix_z = t + 0.5 * (self.zp(t + g) + self.zm(t - g))
        k, dk = coef[0, p], coef[1, p]
        mix = (mix_x, mix_y, mix_z)
        return [dk * u0[c] - k * mix[c] - self.tz(self.ty(b[c])) for c in range(3)]

    def diag(self, k, p):
        t = k[p] + 0.5 * (k[p - 1] + k[p + 1])
        return (3.0 / 7.0) * k[p] + self.tz(self.ty(t)) * (1.0 / 14.0)


def planes_loop(planes, step):
    if isinstance(planes, list):
        low, other, count = planes

        def run(i, carry):
            step(low + i)
            step(other + i)
            return carry

        lax.fori_loop(0, count, run, 0)
        return
    low, high, unroll = planes

    def run(p, carry):
        step(p)
        return carry

    lax.fori_loop(low, high, run, 0, unroll=unroll)


def start_sweep(planes, src, coef, d, v, w):
    def step(p):
        scale = coef[2, p] * (1.0 / MID)
        k = coef[0, p]
        for c in range(3):
            new = src[c, p] * scale
            d[c, p] = new
            v[c, p] = new
            w[c, p] = k * new

    planes_loop(planes, step)


def sweep(plane, planes, factors, src, coef, d, v, w, v_out, w_out):
    alpha, beta = factors

    def step(p):
        image = plane.apply(v, w, coef, p)
        k = coef[0, p]
        scale = coef[2, p] * beta
        for c in range(3):
            new = alpha * d[c, p] + scale * (src[c, p] - image[c])
            d[c, p] = new
            total = v[c, p] + new
            v_out[c, p] = total
            w_out[c, p] = k * total

    planes_loop(planes, step)


def kernel(
    n, loads,
    force, stiff, mat_hbm, face_src_hbm, count_hbm, face_dst_hbm,
    disp_out, sens_out,
    src, raw, coef, d, va, wa, vb, wb, res, pooled, kc, ccoef, csrc, cd, cva, cwa, cvb, cwb,
    mat, face_src, count, face_dst, lane_table, live_table, dst_table,
    wide, sendbuf, arrived, esend, erecv,
    local_sem, send_sem, recv_sem, a_send, a_recv, e_send, e_recv,
):
    me = lax.axis_index("space")
    load = lax.axis_index("load")
    cx, ny, nz = raw.shape
    hx, hy, hz = cx // 2, ny // 2, nz // 2
    fine = Plane(ny, nz)
    coarse = Plane(hy, hz)
    slots = face_src.shape[2]
    top = cx + 2 * FH
    ctop = hx + 2 * CH

    barrier = pltpu.get_barrier_semaphore()

    @pl.loop(1, n)
    def _(k):
        pl.semaphore_signal(
            barrier, inc=1, device_id={"space": lax.rem(me + k, n)}, device_id_type=MESH
        )

    @pl.loop(1, loads)
    def _(k):
        pl.semaphore_signal(
            barrier, inc=1, device_id={"load": lax.rem(load + k, loads)}, device_id_type=MESH
        )

    get_stiff = pltpu.make_async_copy(stiff, raw, local_sem.at[0])
    get_force = pltpu.make_async_copy(force.at[0], src.at[:, pl.ds(FH, cx)], local_sem.at[1])
    get_mat = pltpu.make_async_copy(mat_hbm, mat, local_sem.at[3])
    get_src = pltpu.make_async_copy(face_src_hbm, face_src, local_sem.at[4])
    get_count = pltpu.make_async_copy(count_hbm, count, local_sem.at[5])
    get_dst = pltpu.make_async_copy(face_dst_hbm, face_dst, local_sem.at[6])
    get_stiff.start()
    get_mat.start()
    get_force.start()
    get_src.start()
    get_count.start()
    get_dst.start()

    right = lax.rem(me + 1, n)
    left = lax.rem(me + n - 1, n)

    def pair(kind, to_right, to_left):
        made = []
        for side, (ends, target) in enumerate(((to_right, right), (to_left, left))):
            made.append(
                pltpu.make_async_remote_copy(
                    src_ref=ends[0], dst_ref=ends[1],
                    send_sem=send_sem.at[kind, side], recv_sem=recv_sem.at[kind, side],
                    device_id={"space": target}, device_id_type=MESH,
                )
            )
        return made

    fw = FH - 1
    force_pair = pair(
        0,
        (force.at[0, :, pl.ds(cx - fw, fw)], src.at[:, pl.ds(1, fw)]),
        (force.at[0, :, pl.ds(0, fw)], src.at[:, pl.ds(FH + cx, fw)]),
    )
    coef_pair = pair(
        1,
        (coef.at[0, pl.ds(cx, FH)], coef.at[0, pl.ds(0, FH)]),
        (coef.at[0, pl.ds(FH, FH)], coef.at[0, pl.ds(FH + cx, FH)]),
    )
    ccoef_pair = pair(
        2,
        (ccoef.at[:, pl.ds(CH, hx)], ccoef.at[:, pl.ds(0, hx)]),
        (ccoef.at[:, pl.ds(CH, hx)], ccoef.at[:, pl.ds(CH + hx, hx)]),
    )
    csrc_pair = pair(
        3,
        (csrc.at[:, pl.ds(CH, hx)], csrc.at[:, pl.ds(0, hx)]),
        (csrc.at[:, pl.ds(CH, hx)], csrc.at[:, pl.ds(CH + hx, hx)]),
    )
    has_left, has_right = me > 0, me < n - 1

    def start(made):
        @pl.when(has_right)
        def _():
            made[0].start()

        @pl.when(has_left)
        def _():
            made[1].start()

    def land(made):
        @pl.when(has_left)
        def _():
            made[0].wait_recv()

        @pl.when(has_right)
        def _():
            made[1].wait_recv()

    def sent(made):
        @pl.when(has_right)
        def _():
            made[0].wait_send()

        @pl.when(has_left)
        def _():
            made[1].wait_send()

    @pl.when(me == 0)
    def _():
        src[:, 0:FH] = jnp.zeros((3, FH, ny, nz), F32)
        coef[0, 0:FH] = jnp.zeros((FH, ny, nz), F32)
        ccoef[:, 0:CH] = jnp.zeros((3, CH, hy, hz), F32)
        csrc[:, 0:CH] = jnp.zeros((3, CH, hy, hz), F32)

    @pl.when(me == n - 1)
    def _():
        src[:, FH + cx : top] = jnp.zeros((3, FH, ny, nz), F32)
        coef[0, FH + cx : top] = jnp.zeros((FH, ny, nz), F32)
        ccoef[:, CH + hx : ctop] = jnp.zeros((3, CH, hy, hz), F32)
        csrc[:, CH + hx : ctop] = jnp.zeros((3, CH, hy, hz), F32)

    def by_material(brick, values):
        m = mat[0, brick]
        return jnp.where(m == 0, values[0], jnp.where(m == 1, values[1], values[2]))

    get_mat.wait()
    get_stiff.wait()
    for brick in range(ny // BY):
        own = by_material(brick, MODULI)
        rows = slice(brick * BY, (brick + 1) * BY)
        coef[0, FH : FH + cx, rows] = raw[:, rows] * own

    pl.semaphore_wait(barrier, n - 1 + loads - 1)
    start(coef_pair)
    start(force_pair)

    rows_f = cx * ny
    zbits = nz.bit_length() - 1
    hbits = hz.bit_length() - 1
    get_src.wait()
    get_count.wait()
    get_dst.wait()

    @pl.loop(0, n)
    def _(owner):
        sub_z = lax.broadcasted_iota(jnp.int32, (nz, slots), 0)
        sub_r = lax.broadcasted_iota(jnp.int32, (rows_f, slots), 0)
        slot_r = lax.broadcasted_iota(jnp.int32, (rows_f, slots), 1)
        index = face_src[0, pl.ds(owner, 1), :]
        lane_table[owner] = (sub_z == jnp.bitwise_and(index, nz - 1)).astype(F32).astype(BF16)
        live = jnp.logical_and(
            sub_r == lax.shift_right_logical(index, zbits), slot_r < count[0, owner]
        )
        live_table[owner] = live.astype(F32)
        sub_l = lax.broadcasted_iota(jnp.int32, (hz, slots), 0)
        index = face_dst[0, pl.ds(owner, 1), :]
        dst_table[owner] = (sub_l == jnp.bitwise_and(index, hz - 1)).astype(F32).astype(BF16)

    kview = coef.at[0]

    def diag_step(p):
        diag = fine.diag(kview, p)
        inside = jnp.logical_and(
            jnp.logical_or(p >= FH, has_left), jnp.logical_or(p < FH + cx, has_right)
        )
        keep = jnp.where(inside, 1.0, 0.0)
        coef[1, p] = diag + coef[0, p] * (1.0 / 7.0)
        coef[2, p] = keep / jnp.where(inside, diag, 1.0)

    factors = cheb_factors(FINE_STEPS)
    last = FH + cx
    planes_loop((FH + 1, last - 1, 2), diag_step)
    get_force.wait()
    start_sweep((FH + 1, last - 1, 2), src, coef, d, va, wa)
    sweep(fine, (FH + 2, last - 2, 2), factors[0], src, coef, d, va, wa, vb, wb)
    sweep(fine, (FH + 3, last - 3, 2), factors[1], src, coef, d, vb, wb, va, wa)

    land(coef_pair)
    planes_loop([1, last - 1, FH], diag_step)
    land(force_pair)
    start_sweep([1, last - 1, FH], src, coef, d, va, wa)
    sweep(fine, [2, last - 2, FH], factors[0], src, coef, d, va, wa, vb, wb)
    sweep(fine, [3, last - 3, FH], factors[1], src, coef, d, vb, wb, va, wa)

    def residual_step(p):
        image = fine.apply(va, wa, coef, p)
        for c in range(3):
            part = src[c, p] - image[c]
            res[c, p - FH] = part
            hi, lo = split(part)
            at = pl.ds(pl.multiple_of((p - FH) * ny, ny), ny)
            wide[0, c, at, :] = hi
            wide[1, c, at, :] = lo

    planes_loop((FH, last, 2), residual_step)

    def pick(owner):
        lanes = lane_table[owner]
        live = live_table[owner]
        hi = wide[0].reshape(3 * rows_f, nz)
        lo = wide[1].reshape(3 * rows_f, nz)
        found = jnp.dot(hi, lanes, preferred_element_type=F32) + jnp.dot(
            lo, lanes, preferred_element_type=F32
        )
        rows = [
            jnp.sum(found[c * rows_f : (c + 1) * rows_f] * live, axis=0, keepdims=True)
            for c in range(3)
        ]
        return jnp.concatenate(rows + [jnp.zeros((5, slots), F32)], axis=0)

    def a_copy(k):
        owner = lax.rem(me + k, n)
        return pltpu.make_async_remote_copy(
            src_ref=sendbuf.at[owner], dst_ref=arrived.at[me],
            send_sem=a_send.at[k], recv_sem=a_recv.at[k],
            device_id={"space": owner}, device_id_type=MESH,
        )

    def pick_and_send(k, carry):
        owner = lax.rem(me + k, n)
        sendbuf[owner] = pick(owner)
        a_copy(k).start()
        return carry

    lax.fori_loop(1, n, pick_and_send, 0)
    arrived[me] = pick(me)

    pool = (
        lax.shift_right_logical(lax.broadcasted_iota(jnp.int32, (nz, hz), 0), 1)
        == lax.broadcasted_iota(jnp.int32, (nz, hz), 1)
    ).astype(F32).astype(BF16)
    spread = (
        lax.shift_right_logical(lax.broadcasted_iota(jnp.int32, (hz, nz), 1), 1)
        == lax.broadcasted_iota(jnp.int32, (hz, nz), 0)
    ).astype(F32).astype(BF16)

    def pool_rows(i):
        return pooled[i, pl.ds(0, hy, stride=2), :] + pooled[i, pl.ds(1, hy, stride=2), :]

    count_c = hx + 2
    first = FH - 2
    stack = jnp.concatenate(
        [coef[0, first + 2 * i] + coef[0, first + 2 * i + 1] for i in range(count_c)], axis=0
    )
    pooled[0:count_c] = dot2(stack, pool).reshape(count_c, ny, hz)
    for i in range(count_c):
        kc[i] = pool_rows(i) * 0.125
    for i in range(hx):
        diag = coarse.diag(kc, i + 1)
        ccoef[0, CH + i] = kc[i + 1]
        ccoef[1, CH + i] = diag + kc[i + 1] * (1.0 / 7.0)
        ccoef[2, CH + i] = 1.0 / diag
    start(ccoef_pair)

    for c in range(3):
        stack = jnp.concatenate([res[c, 2 * i] + res[c, 2 * i + 1] for i in range(hx)], axis=0)
        pooled[0:hx] = dot2(stack, pool).reshape(hx, ny, hz)
        for i in range(hx):
            csrc[c, CH + i] = pool_rows(i) * 0.5

    rows_c = hx * hy
    sub_c = lax.broadcasted_iota(jnp.int32, (rows_c, slots), 0)

    def place(sender):
        index = face_dst[0, pl.ds(sender, 1), :]
        lanes = dst_table[sender]
        at_row = sub_c == lax.shift_right_logical(index, hbits)
        values = arrived[sender]
        parts = [jnp.where(at_row, values[c : c + 1], 0.0) for c in range(3)]
        hi, lo = split(jnp.concatenate(parts, axis=0))
        dims = (((1,), (1,)), ((), ()))
        return lax.dot_general(hi, lanes, dims, preferred_element_type=F32) + lax.dot_general(
            lo, lanes, dims, preferred_element_type=F32
        )

    total = place(me)

    @pl.loop(1, n)
    def _(k):
        a_copy(k).wait_recv()

    def add_sender(k, total):
        return total + place(lax.rem(me + n - k, n))

    total = lax.fori_loop(1, n, add_sender, total, unroll=min(n - 1, 7))
    csrc[:, CH : CH + hx] += total.reshape(3, hx, hy, hz)
    start(csrc_pair)
    land(ccoef_pair)
    land(csrc_pair)

    factors = cheb_factors(COARSE_STEPS)
    start_sweep((0, ctop, ctop), csrc, ccoef, cd, cva, cwa)
    sweep(coarse, (1, ctop - 1, ctop - 2), factors[0], csrc, ccoef, cd, cva, cwa, cvb, cwb)
    sweep(coarse, (2, ctop - 2, ctop - 4), factors[1], csrc, ccoef, cd, cvb, cwb, cva, cwa)
    sweep(coarse, (3, ctop - 3, ctop - 6), factors[2], csrc, ccoef, cd, cva, cwa, cvb, cwb)

    fresh = hx + 2
    for c in range(3):
        lifted = dot2(cvb[c, 3 : 3 + fresh].reshape(fresh * hy, hz), spread)
        for i in range(fresh):
            plane = lifted[i * hy : (i + 1) * hy]
            doubled = jnp.broadcast_to(plane[:, None, :], (hy, 2, nz)).reshape(ny, nz)
            for p in (FH - 2 + 2 * i, FH - 1 + 2 * i):
                if FH - 1 <= p <= FH + cx:
                    vb[c, p] = va[c, p] + doubled
                    wb[c, p] = coef[0, p] * vb[c, p]

    put_disp = pltpu.make_async_copy(
        vb.at[:, pl.ds(FH, cx)], disp_out.at[0], local_sem.at[2]
    )
    put_disp.start()

    part = ny // loads

    def energy_step(p):
        image = fine.apply(vb, wb, coef, p)
        energy = vb[0, p] * image[0] + vb[1, p] * image[1] + vb[2, p] * image[2]
        for i in range(loads):
            esend[i, p - FH] = energy[i * part : (i + 1) * part]

    planes_loop((FH, FH + cx, 2), energy_step)

    def e_copy(k):
        owner = lax.rem(load + k, loads)
        return pltpu.make_async_remote_copy(
            src_ref=esend.at[owner], dst_ref=erecv.at[k],
            send_sem=e_send.at[k], recv_sem=e_recv.at[k],
            device_id={"load": owner}, device_id_type=MESH,
        )

    for k in range(1, loads):
        e_copy(k).start()

    sent(force_pair)
    sent(coef_pair)
    sent(ccoef_pair)
    sent(csrc_pair)

    @pl.loop(1, n)
    def _(k):
        a_copy(k).wait_send()

    total = esend[load]
    for k in range(1, loads):
        e_copy(k).wait_recv()
        total = total + erecv[k]
    brick = (load * part) // BY
    for m, modulus in enumerate(MODULI):
        ratio = by_material(brick, [(modulus - own) / own for own in MODULI])
        sens_out[m] = total * ratio
    for k in range(1, loads):
        e_copy(k).wait_send()
    put_disp.wait()


def body(n, loads, load_force, stiffness, material, face_src, face_count, face_dst):
    cx, ny, nz = stiffness.shape
    hx, hy, hz = cx // 2, ny // 2, nz // 2
    slots = face_src.shape[2]
    part = ny // loads
    fine = (cx + 2 * FH, ny, nz)
    coarse = (hx + 2 * CH, hy, hz)
    vmem = pl.BlockSpec(memory_space=pltpu.VMEM)
    hbm = pl.BlockSpec(memory_space=pltpu.HBM)

    def buf(*shape):
        return pltpu.VMEM(shape, F32)

    dma = pltpu.SemaphoreType.DMA
    return pl.pallas_call(
        functools.partial(kernel, n, loads),
        out_shape=(
            jax.ShapeDtypeStruct(load_force.shape, F32),
            jax.ShapeDtypeStruct((3, cx, part, nz), F32),
        ),
        in_specs=[hbm] * 6,
        out_specs=(hbm, vmem),
        scratch_shapes=[
            buf(3, *fine), buf(cx, ny, nz), buf(3, *fine), buf(3, *fine),
            buf(3, *fine), buf(3, *fine), buf(3, *fine), buf(3, *fine),
            buf(3, cx, ny, nz), buf(hx + 2, ny, hz), buf(hx + 2, hy, hz),
            buf(3, *coarse), buf(3, *coarse), buf(3, *coarse),
            buf(3, *coarse), buf(3, *coarse), buf(3, *coarse), buf(3, *coarse),
            pltpu.SMEM(material.shape, jnp.int32), pltpu.VMEM(face_src.shape, jnp.int32),
            pltpu.SMEM(face_count.shape, jnp.int32), pltpu.VMEM(face_dst.shape, jnp.int32),
            pltpu.VMEM((n, nz, slots), BF16), buf(n, cx * ny, slots),
            pltpu.VMEM((n, hz, slots), BF16),
            pltpu.VMEM((2, 3, cx * ny, nz), BF16),
            buf(n, 8, slots), buf(n, 8, slots),
            buf(loads, cx, part, nz), buf(loads, cx, part, nz),
            dma((7,)), dma((4, 2)), dma((4, 2)),
            dma((n,)), dma((n,)), dma((loads,)), dma((loads,)),
        ],
        compiler_params=pltpu.CompilerParams(
            collective_id=0, has_side_effects=True, vmem_limit_bytes=60 * 1024 * 1024
        ),
    )(load_force, stiffness, material, face_src, face_count, face_dst)


def solution(mesh):
    return jax.shard_map(
        functools.partial(body, mesh.shape["space"], mesh.shape["load"]),
        mesh=mesh,
        in_specs=(
            P("load", None, "space", None, None),
            P("space", None, None),
            P("space", None),
            P("space", None, None),
            P("space", None),
            P("space", None, None),
        ),
        out_specs=(P("load", None, "space", None, None), P(None, "space", "load", None)),
        check_vma=False,
    )
```

```python
import functools

import jax
import jax.numpy as jnp
from jax import lax
from jax.experimental import pallas as pl
from jax.experimental.pallas import tpu as pltpu
from jax.sharding import PartitionSpec as P

BY = 8
FINE_STEPS = 3
COARSE_STEPS = 4
UPPER_EDGE = 2.1
LOWER_EDGE = 0.15
COUPLING = 0.1
MODULI = (1.0, 0.55, 0.25)

MID = (UPPER_EDGE + LOWER_EDGE) / 2.0
HALF = (UPPER_EDGE - LOWER_EDGE) / 2.0
F32 = jnp.float32
BF16 = jnp.bfloat16
MESH = pl.DeviceIdType.MESH
FH = 4
CH = 4


def cheb_factors(count):
    spread = MID / HALF
    rho = 1.0 / spread
    out = []
    for _ in range(1, count):
        rho_new = 1.0 / (2.0 * spread - rho)
        out.append((rho_new * rho, 2.0 * rho_new / HALF))
        rho = rho_new
    return out


def split(x):
    hi = x.astype(BF16)
    return hi, (x - hi.astype(F32)).astype(BF16)


def dot2(x, table):
    hi, lo = split(x)
    return jnp.dot(hi, table, preferred_element_type=F32) + jnp.dot(
        lo, table, preferred_element_type=F32
    )


class Plane:
    def __init__(self, rows, lanes):
        self.sizes = (rows, lanes)
        self.masks = []
        for axis, other in ((0, lanes), (1, rows)):
            shape = (8, other) if axis == 0 else (other, 128)
            place = lax.broadcasted_iota(jnp.int32, shape, axis)
            self.masks.append((place == shape[axis] - 1, place == 0))

    def shift(self, a, axis, up):
        tile = (8, 128)[axis]
        count = self.sizes[axis] // tile
        mask = self.masks[axis][0 if up else 1]
        turned = [
            pltpu.roll(
                lax.slice_in_dim(a, i * tile, (i + 1) * tile, axis=axis),
                tile - 1 if up else 1,
                axis,
            )
            for i in range(count)
        ]
        out = []
        for i in range(count):
            near = i + 1 if up else i - 1
            fill = turned[near] if 0 <= near < count else 0.0
            out.append(jnp.where(mask, fill, turned[i]))
        return out[0] if count == 1 else jnp.concatenate(out, axis=axis)

    def yp(self, a):
        return self.shift(a, 0, True)

    def ym(self, a):
        return self.shift(a, 0, False)

    def zp(self, a):
        return self.shift(a, 1, True)

    def zm(self, a):
        return self.shift(a, 1, False)

    def ty(self, a):
        return a + 0.5 * (self.yp(a) + self.ym(a))

    def tz(self, a):
        return a + 0.5 * (self.zp(a) + self.zm(a))

    def apply(self, v, w, coef, p):
        u0 = [v[c, p] for c in range(3)]
        um = [v[c, p - 1] for c in range(3)]
        up = [v[c, p + 1] for c in range(3)]
        a = [(u0[c] + 0.5 * (um[c] + up[c])) * (1.0 / 14.0) for c in range(3)]
        e = [(up[c] - um[c]) * (0.5 * COUPLING) for c in range(3)]
        b = [(w[c, p] + 0.5 * (w[c, p - 1] + w[c, p + 1])) * (1.0 / 14.0) for c in range(3)]
        half = 0.5 * COUPLING
        t = self.ty(a[0])
        mix_x = (
            t
            + 0.5 * (self.zp(t + e[2]) + self.zm(t - e[2]))
            + 0.5 * (self.yp(e[1]) - self.ym(e[1]))
        )
        t = self.tz(a[1])
        g = e[0] + half * (self.zp(u0[2]) - self.zm(u0[2]))
        mix_y = t + 0.5 * (self.yp(t + g) + self.ym(t - g))
        t = self.ty(a[2])
        g = e[0] + half * (self.yp(u0[1]) - self.ym(u0[1]))
        mix_z = t + 0.5 * (self.zp(t + g) + self.zm(t - g))
        k, dk = coef[0, p], coef[1, p]
        mix = (mix_x, mix_y, mix_z)
        return [dk * u0[c] - k * mix[c] - self.tz(self.ty(b[c])) for c in range(3)]

    def diag(self, k, p):
        t = k[p] + 0.5 * (k[p - 1] + k[p + 1])
        return (3.0 / 7.0) * k[p] + self.tz(self.ty(t)) * (1.0 / 14.0)


def planes_loop(planes, step):
    if isinstance(planes, list):
        low, other, count = planes

        def run(i, carry):
            step(low + i)
            step(other + i)
            return carry

        lax.fori_loop(0, count, run, 0)
        return
    low, high, unroll = planes

    def run(p, carry):
        step(p)
        return carry

    lax.fori_loop(low, high, run, 0, unroll=unroll)


def start_sweep(planes, src, coef, d, v, w):
    def step(p):
        scale = coef[2, p] * (1.0 / MID)
        k = coef[0, p]
        for c in range(3):
            new = src[c, p] * scale
            d[c, p] = new
            v[c, p] = new
            w[c, p] = k * new

    planes_loop(planes, step)


def sweep(plane, planes, factors, src, coef, d, v, w, v_out, w_out):
    alpha, beta = factors

    def step(p):
        image = plane.apply(v, w, coef, p)
        k = coef[0, p]
        scale = coef[2, p] * beta
        for c in range(3):
            new = alpha * d[c, p] + scale * (src[c, p] - image[c])
            d[c, p] = new
            total = v[c, p] + new
            v_out[c, p] = total
            w_out[c, p] = k * total

    planes_loop(planes, step)


def kernel(
    n, loads,
    force, stiff, mat_hbm, face_src_hbm, count_hbm, face_dst_hbm,
    disp_out, sens_out,
    src, raw, coef, d, va, wa, vb, wb, res, pooled, kc, ccoef, csrc, cd, cva, cwa, cvb, cwb,
    mat, face_src, count, face_dst, lane_table, live_table, dst_table,
    wide, sendbuf, arrived, esend, erecv,
    local_sem, send_sem, recv_sem, a_send, a_recv, e_send, e_recv,
):
    me = lax.axis_index("space")
    load = lax.axis_index("load")
    cx, ny, nz = raw.shape
    hx, hy, hz = cx // 2, ny // 2, nz // 2
    fine = Plane(ny, nz)
    coarse = Plane(hy, hz)
    slots = face_src.shape[2]
    top = cx + 2 * FH
    ctop = hx + 2 * CH

    barrier = pltpu.get_barrier_semaphore()

    @pl.loop(1, n)
    def _(k):
        pl.semaphore_signal(
            barrier, inc=1, device_id={"space": lax.rem(me + k, n)}, device_id_type=MESH
        )

    @pl.loop(1, loads)
    def _(k):
        pl.semaphore_signal(
            barrier, inc=1, device_id={"load": lax.rem(load + k, loads)}, device_id_type=MESH
        )

    get_stiff = pltpu.make_async_copy(stiff, raw, local_sem.at[0])
    get_force = pltpu.make_async_copy(force.at[0], src.at[:, pl.ds(FH, cx)], local_sem.at[1])
    get_mat = pltpu.make_async_copy(mat_hbm, mat, local_sem.at[3])
    get_src = pltpu.make_async_copy(face_src_hbm, face_src, local_sem.at[4])
    get_count = pltpu.make_async_copy(count_hbm, count, local_sem.at[5])
    get_dst = pltpu.make_async_copy(face_dst_hbm, face_dst, local_sem.at[6])
    get_stiff.start()
    get_mat.start()
    get_force.start()
    get_src.start()
    get_count.start()
    get_dst.start()

    right = lax.rem(me + 1, n)
    left = lax.rem(me + n - 1, n)

    def pair(kind, to_right, to_left):
        made = []
        for side, (ends, target) in enumerate(((to_right, right), (to_left, left))):
            made.append(
                pltpu.make_async_remote_copy(
                    src_ref=ends[0], dst_ref=ends[1],
                    send_sem=send_sem.at[kind, side], recv_sem=recv_sem.at[kind, side],
                    device_id={"space": target}, device_id_type=MESH,
                )
            )
        return made

    fw = FH - 1
    force_pair = pair(
        0,
        (force.at[0, :, pl.ds(cx - fw, fw)], src.at[:, pl.ds(1, fw)]),
        (force.at[0, :, pl.ds(0, fw)], src.at[:, pl.ds(FH + cx, fw)]),
    )
    coef_pair = pair(
        1,
        (coef.at[0, pl.ds(cx, FH)], coef.at[0, pl.ds(0, FH)]),
        (coef.at[0, pl.ds(FH, FH)], coef.at[0, pl.ds(FH + cx, FH)]),
    )
    ccoef_pair = pair(
        2,
        (ccoef.at[:, pl.ds(CH, hx)], ccoef.at[:, pl.ds(0, hx)]),
        (ccoef.at[:, pl.ds(CH, hx)], ccoef.at[:, pl.ds(CH + hx, hx)]),
    )
    csrc_pair = pair(
        3,
        (csrc.at[:, pl.ds(CH, hx)], csrc.at[:, pl.ds(0, hx)]),
        (csrc.at[:, pl.ds(CH, hx)], csrc.at[:, pl.ds(CH + hx, hx)]),
    )
    has_left, has_right = me > 0, me < n - 1

    def start(made):
        @pl.when(has_right)
        def _():
            made[0].start()

        @pl.when(has_left)
        def _():
            made[1].start()

    def land(made):
        @pl.when(has_left)
        def _():
            made[0].wait_recv()

        @pl.when(has_right)
        def _():
            made[1].wait_recv()

    def sent(made):
        @pl.when(has_right)
        def _():
            made[0].wait_send()

        @pl.when(has_left)
        def _():
            made[1].wait_send()

    @pl.when(me == 0)
    def _():
        src[:, 0:FH] = jnp.zeros((3, FH, ny, nz), F32)
        coef[0, 0:FH] = jnp.zeros((FH, ny, nz), F32)
        ccoef[:, 0:CH] = jnp.zeros((3, CH, hy, hz), F32)
        csrc[:, 0:CH] = jnp.zeros((3, CH, hy, hz), F32)

    @pl.when(me == n - 1)
    def _():
        src[:, FH + cx : top] = jnp.zeros((3, FH, ny, nz), F32)
        coef[0, FH + cx : top] = jnp.zeros((FH, ny, nz), F32)
        ccoef[:, CH + hx : ctop] = jnp.zeros((3, CH, hy, hz), F32)
        csrc[:, CH + hx : ctop] = jnp.zeros((3, CH, hy, hz), F32)

    def by_material(brick, values):
        m = mat[0, brick]
        return jnp.where(m == 0, values[0], jnp.where(m == 1, values[1], values[2]))

    get_mat.wait()
    get_stiff.wait()
    for brick in range(ny // BY):
        own = by_material(brick, MODULI)
        rows = slice(brick * BY, (brick + 1) * BY)
        coef[0, FH : FH + cx, rows] = raw[:, rows] * own

    pl.semaphore_wait(barrier, n - 1 + loads - 1)
    start(coef_pair)
    start(force_pair)

    rows_f = cx * ny
    zbits = nz.bit_length() - 1
    hbits = hz.bit_length() - 1
    get_src.wait()
    get_count.wait()
    get_dst.wait()

    @pl.loop(0, n)
    def _(owner):
        sub_z = lax.broadcasted_iota(jnp.int32, (nz, slots), 0)
        sub_r = lax.broadcasted_iota(jnp.int32, (rows_f, slots), 0)
        slot_r = lax.broadcasted_iota(jnp.int32, (rows_f, slots), 1)
        index = face_src[0, pl.ds(owner, 1), :]
        lanes = (sub_z == jnp.bitwise_and(index, nz - 1)).astype(F32).astype(BF16)
        lane_table[owner, 0:nz] = lanes
        lane_table[owner, nz : 2 * nz] = lanes
        live = jnp.logical_and(
            sub_r == lax.shift_right_logical(index, zbits), slot_r < count[0, owner]
        )
        live_table[owner] = live.astype(F32)
        sub_l = lax.broadcasted_iota(jnp.int32, (hz, slots), 0)
        index = face_dst[0, pl.ds(owner, 1), :]
        dst_table[owner] = (sub_l == jnp.bitwise_and(index, hz - 1)).astype(F32).astype(BF16)

    kview = coef.at[0]

    def diag_step(p):
        diag = fine.diag(kview, p)
        inside = jnp.logical_and(
            jnp.logical_or(p >= FH, has_left), jnp.logical_or(p < FH + cx, has_right)
        )
        keep = jnp.where(inside, 1.0, 0.0)
        coef[1, p] = diag + coef[0, p] * (1.0 / 7.0)
        coef[2, p] = keep / jnp.where(inside, diag, 1.0)

    factors = cheb_factors(FINE_STEPS)
    last = FH + cx
    planes_loop((FH + 1, last - 1, 2), diag_step)
    get_force.wait()
    start_sweep((FH + 1, last - 1, 2), src, coef, d, va, wa)
    sweep(fine, (FH + 2, last - 2, 2), factors[0], src, coef, d, va, wa, vb, wb)
    sweep(fine, (FH + 3, last - 3, 2), factors[1], src, coef, d, vb, wb, va, wa)

    land(coef_pair)
    planes_loop([1, last - 1, FH], diag_step)
    land(force_pair)
    start_sweep([1, last - 1, FH], src, coef, d, va, wa)
    sweep(fine, [2, last - 2, FH], factors[0], src, coef, d, va, wa, vb, wb)
    sweep(fine, [3, last - 3, FH], factors[1], src, coef, d, vb, wb, va, wa)

    def residual_step(p):
        image = fine.apply(va, wa, coef, p)
        for c in range(3):
            part = src[c, p] - image[c]
            res[c, p - FH] = part
            hi, lo = split(part)
            at = pl.ds(pl.multiple_of((p - FH) * ny, ny), ny)
            wide[c, at, 0:nz] = hi
            wide[c, at, nz : 2 * nz] = lo

    planes_loop((FH, last, 2), residual_step)

    def pick(owner):
        live = live_table[owner]
        found = jnp.dot(
            wide[...].reshape(3 * rows_f, 2 * nz), lane_table[owner], preferred_element_type=F32
        )
        rows = [
            jnp.sum(found[c * rows_f : (c + 1) * rows_f] * live, axis=0, keepdims=True)
            for c in range(3)
        ]
        return jnp.concatenate(rows + [jnp.zeros((5, slots), F32)], axis=0)

    def a_copy(k):
        owner = lax.rem(me + k, n)
        return pltpu.make_async_remote_copy(
            src_ref=sendbuf.at[owner], dst_ref=arrived.at[me],
            send_sem=a_send.at[k], recv_sem=a_recv.at[k],
            device_id={"space": owner}, device_id_type=MESH,
        )

    group = 4 if n % 4 == 0 else 1

    @pl.loop(0, n // group)
    def _(i):
        ks = [i * group + 1 + j for j in range(group)]
        picked = [pick(lax.rem(me + k, n)) for k in ks]
        for k, values in zip(ks, picked):
            sendbuf[lax.rem(me + k, n)] = values
        for k in ks:

            @pl.when(k < n)
            def _(k=k):
                a_copy(k).start()

    arrived[me] = sendbuf[me]

    pool = (
        lax.shift_right_logical(lax.broadcasted_iota(jnp.int32, (nz, hz), 0), 1)
        == lax.broadcasted_iota(jnp.int32, (nz, hz), 1)
    ).astype(F32).astype(BF16)
    spread = (
        lax.shift_right_logical(lax.broadcasted_iota(jnp.int32, (hz, nz), 1), 1)
        == lax.broadcasted_iota(jnp.int32, (hz, nz), 0)
    ).astype(F32).astype(BF16)

    def pool_rows(i):
        return pooled[i, pl.ds(0, hy, stride=2), :] + pooled[i, pl.ds(1, hy, stride=2), :]

    count_c = hx + 2
    first = FH - 2
    stack = jnp.concatenate(
        [coef[0, first + 2 * i] + coef[0, first + 2 * i + 1] for i in range(count_c)], axis=0
    )
    pooled[0:count_c] = dot2(stack, pool).reshape(count_c, ny, hz)
    for i in range(count_c):
        kc[i] = pool_rows(i) * 0.125
    for i in range(hx):
        diag = coarse.diag(kc, i + 1)
        ccoef[0, CH + i] = kc[i + 1]
        ccoef[1, CH + i] = diag + kc[i + 1] * (1.0 / 7.0)
        ccoef[2, CH + i] = 1.0 / diag
    start(ccoef_pair)

    for c in range(3):
        stack = jnp.concatenate([res[c, 2 * i] + res[c, 2 * i + 1] for i in range(hx)], axis=0)
        pooled[0:hx] = dot2(stack, pool).reshape(hx, ny, hz)
        for i in range(hx):
            csrc[c, CH + i] = pool_rows(i) * 0.5

    rows_c = hx * hy
    sub_c = lax.broadcasted_iota(jnp.int32, (rows_c, slots), 0)

    def place(sender):
        index = face_dst[0, pl.ds(sender, 1), :]
        lanes = dst_table[sender]
        at_row = sub_c == lax.shift_right_logical(index, hbits)
        values = arrived[sender]
        parts = [jnp.where(at_row, values[c : c + 1], 0.0) for c in range(3)]
        hi, lo = split(jnp.concatenate(parts, axis=0))
        dims = (((1,), (1,)), ((), ()))
        return lax.dot_general(hi, lanes, dims, preferred_element_type=F32) + lax.dot_general(
            lo, lanes, dims, preferred_element_type=F32
        )

    total = place(me)

    @pl.loop(1, n)
    def _(k):
        a_copy(k).wait_recv()

    def add_sender(k, total):
        return total + place(lax.rem(me + n - k, n))

    total = lax.fori_loop(1, n, add_sender, total, unroll=min(n - 1, 7))
    csrc[:, CH : CH + hx] += total.reshape(3, hx, hy, hz)
    start(csrc_pair)
    land(ccoef_pair)
    land(csrc_pair)

    factors = cheb_factors(COARSE_STEPS)
    start_sweep((0, ctop, ctop), csrc, ccoef, cd, cva, cwa)
    sweep(coarse, (1, ctop - 1, ctop - 2), factors[0], csrc, ccoef, cd, cva, cwa, cvb, cwb)
    sweep(coarse, (2, ctop - 2, ctop - 4), factors[1], csrc, ccoef, cd, cvb, cwb, cva, cwa)
    sweep(coarse, (3, ctop - 3, ctop - 6), factors[2], csrc, ccoef, cd, cva, cwa, cvb, cwb)

    fresh = hx + 2
    for c in range(3):
        lifted = dot2(cvb[c, 3 : 3 + fresh].reshape(fresh * hy, hz), spread)
        for i in range(fresh):
            plane = lifted[i * hy : (i + 1) * hy]
            doubled = jnp.broadcast_to(plane[:, None, :], (hy, 2, nz)).reshape(ny, nz)
            for p in (FH - 2 + 2 * i, FH - 1 + 2 * i):
                if FH - 1 <= p <= FH + cx:
                    vb[c, p] = va[c, p] + doubled
                    wb[c, p] = coef[0, p] * vb[c, p]

    put_disp = pltpu.make_async_copy(
        vb.at[:, pl.ds(FH, cx)], disp_out.at[0], local_sem.at[2]
    )
    put_disp.start()

    part = ny // loads

    def energy_step(p):
        image = fine.apply(vb, wb, coef, p)
        energy = vb[0, p] * image[0] + vb[1, p] * image[1] + vb[2, p] * image[2]
        for i in range(loads):
            esend[i, p - FH] = energy[i * part : (i + 1) * part]

    halves = 2
    chunk = cx // halves

    def e_copy(k, half):
        owner = lax.rem(load + k, loads)
        return pltpu.make_async_remote_copy(
            src_ref=esend.at[owner, pl.ds(half * chunk, chunk)],
            dst_ref=erecv.at[k, pl.ds(half * chunk, chunk)],
            send_sem=e_send.at[k, half], recv_sem=e_recv.at[k, half],
            device_id={"load": owner}, device_id_type=MESH,
        )

    for half in range(halves):
        planes_loop((FH + half * chunk, FH + (half + 1) * chunk, 2), energy_step)
        for k in range(1, loads):
            e_copy(k, half).start()

    sent(force_pair)
    sent(coef_pair)
    sent(ccoef_pair)
    sent(csrc_pair)

    @pl.loop(1, n)
    def _(k):
        a_copy(k).wait_send()

    brick = (load * part) // BY
    ratios = [by_material(brick, [(modulus - own) / own for own in MODULI]) for modulus in MODULI]
    put_disp.wait()
    for half in range(halves):
        rows = slice(half * chunk, (half + 1) * chunk)
        total = esend[load, rows]
        for k in range(1, loads):
            e_copy(k, half).wait_recv()
            total = total + erecv[k, rows]
        for m in range(len(MODULI)):
            sens_out[m, rows] = total * ratios[m]
    for half in range(halves):
        for k in range(1, loads):
            e_copy(k, half).wait_send()


def deliver(disp, sens, disp_out, sens_out, sems):
    copies = [
        pltpu.make_async_copy(disp.at[0, c], disp_out.at[0, c], sems.at[c]) for c in range(3)
    ]
    copies.append(pltpu.make_async_copy(sens, sens_out, sems.at[3]))
    for copy in copies:
        copy.start()
    for copy in copies:
        copy.wait()


def body(n, loads, load_force, stiffness, material, face_src, face_count, face_dst):
    cx, ny, nz = stiffness.shape
    hx, hy, hz = cx // 2, ny // 2, nz // 2
    slots = face_src.shape[2]
    part = ny // loads
    fine = (cx + 2 * FH, ny, nz)
    coarse = (hx + 2 * CH, hy, hz)
    vmem = pl.BlockSpec(memory_space=pltpu.VMEM)
    hbm = pl.BlockSpec(memory_space=pltpu.HBM)

    def buf(*shape):
        return pltpu.VMEM(shape, F32)

    dma = pltpu.SemaphoreType.DMA
    disp, sens = pl.pallas_call(
        functools.partial(kernel, n, loads),
        out_shape=(
            jax.ShapeDtypeStruct(load_force.shape, F32),
            jax.ShapeDtypeStruct((3, cx, part, nz), F32),
        ),
        in_specs=[hbm] * 6,
        out_specs=(hbm, vmem),
        scratch_shapes=[
            buf(3, *fine), buf(cx, ny, nz), buf(3, *fine), buf(3, *fine),
            buf(3, *fine), buf(3, *fine), buf(3, *fine), buf(3, *fine),
            buf(3, cx, ny, nz), buf(hx + 2, ny, hz), buf(hx + 2, hy, hz),
            buf(3, *coarse), buf(3, *coarse), buf(3, *coarse),
            buf(3, *coarse), buf(3, *coarse), buf(3, *coarse), buf(3, *coarse),
            pltpu.SMEM(material.shape, jnp.int32), pltpu.VMEM(face_src.shape, jnp.int32),
            pltpu.SMEM(face_count.shape, jnp.int32), pltpu.VMEM(face_dst.shape, jnp.int32),
            pltpu.VMEM((n, 2 * nz, slots), BF16), buf(n, cx * ny, slots),
            pltpu.VMEM((n, hz, slots), BF16),
            pltpu.VMEM((3, cx * ny, 2 * nz), BF16),
            buf(n, 8, slots), buf(n, 8, slots),
            buf(loads, cx, part, nz), buf(loads, cx, part, nz),
            dma((7,)), dma((4, 2)), dma((4, 2)),
            dma((n,)), dma((n,)), dma((loads, 2)), dma((loads, 2)),
        ],
        compiler_params=pltpu.CompilerParams(
            collective_id=0, has_side_effects=True, vmem_limit_bytes=60 * 1024 * 1024
        ),
    )(load_force, stiffness, material, face_src, face_count, face_dst)
    return pl.pallas_call(
        deliver,
        out_shape=(
            jax.ShapeDtypeStruct(disp.shape, F32),
            jax.ShapeDtypeStruct(sens.shape, F32),
        ),
        in_specs=[hbm] * 2,
        out_specs=(hbm, hbm),
        scratch_shapes=[dma((4,))],
        compiler_params=pltpu.CompilerParams(vmem_limit_bytes=60 * 1024 * 1024),
    )(disp, sens)


def solution(mesh):
    return jax.shard_map(
        functools.partial(body, mesh.shape["space"], mesh.shape["load"]),
        mesh=mesh,
        in_specs=(
            P("load", None, "space", None, None),
            P("space", None, None),
            P("space", None),
            P("space", None, None),
            P("space", None),
            P("space", None, None),
        ),
        out_specs=(P("load", None, "space", None, None), P(None, "space", "load", None)),
        check_vma=False,
    )
```

```python
import functools

import jax
import jax.numpy as jnp
from jax import lax
from jax.experimental import pallas as pl
from jax.experimental.pallas import tpu as pltpu
from jax.sharding import PartitionSpec as P

BY = 8
FINE_STEPS = 3
COARSE_STEPS = 4
UPPER_EDGE = 2.1
LOWER_EDGE = 0.15
COUPLING = 0.1
MODULI = (1.0, 0.55, 0.25)

MID = (UPPER_EDGE + LOWER_EDGE) / 2.0
HALF = (UPPER_EDGE - LOWER_EDGE) / 2.0
F32 = jnp.float32
BF16 = jnp.bfloat16
MESH = pl.DeviceIdType.MESH
FH = 4
CH = 4


def cheb_factors(count):
    spread = MID / HALF
    rho = 1.0 / spread
    out = []
    for _ in range(1, count):
        rho_new = 1.0 / (2.0 * spread - rho)
        out.append((rho_new * rho, 2.0 * rho_new / HALF))
        rho = rho_new
    return out


def split(x):
    hi = x.astype(BF16)
    return hi, (x - hi.astype(F32)).astype(BF16)


def dot2(x, table):
    hi, lo = split(x)
    return jnp.dot(hi, table, preferred_element_type=F32) + jnp.dot(
        lo, table, preferred_element_type=F32
    )


class Plane:
    def __init__(self, rows, lanes):
        self.sizes = (rows, lanes)
        self.masks = []
        for axis, other in ((0, lanes), (1, rows)):
            shape = (8, other) if axis == 0 else (other, 128)
            place = lax.broadcasted_iota(jnp.int32, shape, axis)
            self.masks.append((place == shape[axis] - 1, place == 0))

    def shift(self, a, axis, up):
        tile = (8, 128)[axis]
        count = self.sizes[axis] // tile
        mask = self.masks[axis][0 if up else 1]
        turned = [
            pltpu.roll(
                lax.slice_in_dim(a, i * tile, (i + 1) * tile, axis=axis),
                tile - 1 if up else 1,
                axis,
            )
            for i in range(count)
        ]
        out = []
        for i in range(count):
            near = i + 1 if up else i - 1
            fill = turned[near] if 0 <= near < count else 0.0
            out.append(jnp.where(mask, fill, turned[i]))
        return out[0] if count == 1 else jnp.concatenate(out, axis=axis)

    def yp(self, a):
        return self.shift(a, 0, True)

    def ym(self, a):
        return self.shift(a, 0, False)

    def zp(self, a):
        return self.shift(a, 1, True)

    def zm(self, a):
        return self.shift(a, 1, False)

    def ty(self, a):
        return a + 0.5 * (self.yp(a) + self.ym(a))

    def tz(self, a):
        return a + 0.5 * (self.zp(a) + self.zm(a))

    def apply(self, v, w, coef, p):
        u0 = [v[c, p] for c in range(3)]
        um = [v[c, p - 1] for c in range(3)]
        up = [v[c, p + 1] for c in range(3)]
        a = [(u0[c] + 0.5 * (um[c] + up[c])) * (1.0 / 14.0) for c in range(3)]
        e = [(up[c] - um[c]) * (0.5 * COUPLING) for c in range(3)]
        b = [(w[c, p] + 0.5 * (w[c, p - 1] + w[c, p + 1])) * (1.0 / 14.0) for c in range(3)]
        half = 0.5 * COUPLING
        t = self.ty(a[0])
        mix_x = (
            t
            + 0.5 * (self.zp(t + e[2]) + self.zm(t - e[2]))
            + 0.5 * (self.yp(e[1]) - self.ym(e[1]))
        )
        t = self.tz(a[1])
        g = e[0] + half * (self.zp(u0[2]) - self.zm(u0[2]))
        mix_y = t + 0.5 * (self.yp(t + g) + self.ym(t - g))
        t = self.ty(a[2])
        g = e[0] + half * (self.yp(u0[1]) - self.ym(u0[1]))
        mix_z = t + 0.5 * (self.zp(t + g) + self.zm(t - g))
        k, dk = coef[0, p], coef[1, p]
        mix = (mix_x, mix_y, mix_z)
        return [dk * u0[c] - k * mix[c] - self.tz(self.ty(b[c])) for c in range(3)]

    def diag(self, k, p):
        t = k[p] + 0.5 * (k[p - 1] + k[p + 1])
        return (3.0 / 7.0) * k[p] + self.tz(self.ty(t)) * (1.0 / 14.0)


def planes_loop(planes, step):
    if isinstance(planes, list):
        low, other, count = planes

        def run(i, carry):
            step(low + i)
            step(other + i)
            return carry

        lax.fori_loop(0, count, run, 0)
        return
    low, high, unroll = planes

    def run(p, carry):
        step(p)
        return carry

    lax.fori_loop(low, high, run, 0, unroll=unroll)


def start_sweep(planes, src, coef, d, v, w):
    def step(p):
        scale = coef[2, p] * (1.0 / MID)
        k = coef[0, p]
        for c in range(3):
            new = src[c, p] * scale
            d[c, p] = new
            v[c, p] = new
            w[c, p] = k * new

    planes_loop(planes, step)


def sweep(plane, planes, factors, src, coef, d, v, w, v_out, w_out):
    alpha, beta = factors

    def step(p):
        image = plane.apply(v, w, coef, p)
        k = coef[0, p]
        scale = coef[2, p] * beta
        for c in range(3):
            new = alpha * d[c, p] + scale * (src[c, p] - image[c])
            d[c, p] = new
            total = v[c, p] + new
            v_out[c, p] = total
            w_out[c, p] = k * total

    planes_loop(planes, step)


def kernel(
    n, loads,
    force, stiff, mat_hbm, face_src_hbm, count_hbm, face_dst_hbm,
    disp_out, sens_out,
    src, raw, coef, d, va, wa, vb, wb, res, pooled, kc, kcx, ccoef, csrc, cd, cva, cwa, cvb, cwb,
    lift, mat, face_src, count, face_dst, lane_table, live_table, dst_table,
    wide, sendbuf, arrived, esend, erecv,
    local_sem, send_sem, recv_sem, a_send, a_recv, e_send, e_recv,
):
    me = lax.axis_index("space")
    load = lax.axis_index("load")
    cx, ny, nz = raw.shape
    hx, hy, hz = cx // 2, ny // 2, nz // 2
    fine = Plane(ny, nz)
    coarse = Plane(hy, hz)
    slots = face_src.shape[2]
    top = cx + 2 * FH
    ctop = hx + 2 * CH

    barrier = pltpu.get_barrier_semaphore()

    @pl.loop(1, n)
    def _(k):
        pl.semaphore_signal(
            barrier, inc=1, device_id={"space": lax.rem(me + k, n)}, device_id_type=MESH
        )

    @pl.loop(1, loads)
    def _(k):
        pl.semaphore_signal(
            barrier, inc=1, device_id={"load": lax.rem(load + k, loads)}, device_id_type=MESH
        )

    get_stiff = pltpu.make_async_copy(stiff, raw, local_sem.at[0])
    get_force = pltpu.make_async_copy(force.at[0], src.at[:, pl.ds(FH, cx)], local_sem.at[1])
    get_mat = pltpu.make_async_copy(mat_hbm, mat, local_sem.at[3])
    get_src = pltpu.make_async_copy(face_src_hbm, face_src, local_sem.at[4])
    get_count = pltpu.make_async_copy(count_hbm, count, local_sem.at[5])
    get_dst = pltpu.make_async_copy(face_dst_hbm, face_dst, local_sem.at[6])
    get_stiff.start()
    get_mat.start()
    get_force.start()
    get_src.start()
    get_count.start()
    get_dst.start()

    right = lax.rem(me + 1, n)
    left = lax.rem(me + n - 1, n)

    def pair(kind, to_right, to_left):
        made = []
        for side, (ends, target) in enumerate(((to_right, right), (to_left, left))):
            made.append(
                pltpu.make_async_remote_copy(
                    src_ref=ends[0], dst_ref=ends[1],
                    send_sem=send_sem.at[kind, side], recv_sem=recv_sem.at[kind, side],
                    device_id={"space": target}, device_id_type=MESH,
                )
            )
        return made

    far = FH - 2
    near_pair = pair(
        0,
        (src.at[:, pl.ds(FH + cx - 1, 1)], src.at[:, pl.ds(FH - 1, 1)]),
        (src.at[:, pl.ds(FH, 1)], src.at[:, pl.ds(FH + cx, 1)]),
    )
    far_pair = pair(
        4,
        (src.at[:, pl.ds(FH + cx - 1 - far, far)], src.at[:, pl.ds(1, far)]),
        (src.at[:, pl.ds(FH + 1, far)], src.at[:, pl.ds(FH + cx + 1, far)]),
    )
    coef_pair = pair(
        1,
        (coef.at[0, pl.ds(cx, FH)], coef.at[0, pl.ds(0, FH)]),
        (coef.at[0, pl.ds(FH, FH)], coef.at[0, pl.ds(FH + cx, FH)]),
    )
    kc_pair = pair(
        2,
        (kc.at[pl.ds(0, hx + 1)], kcx.at[pl.ds(0, hx + 1)]),
        (kc.at[pl.ds(1, hx + 1)], kcx.at[pl.ds(CH + 1 + hx, hx + 1)]),
    )
    csrc_pair = pair(
        3,
        (csrc.at[:, pl.ds(CH, hx)], csrc.at[:, pl.ds(0, hx)]),
        (csrc.at[:, pl.ds(CH, hx)], csrc.at[:, pl.ds(CH + hx, hx)]),
    )
    has_left, has_right = me > 0, me < n - 1

    def start(made):
        @pl.when(has_right)
        def _():
            made[0].start()

        @pl.when(has_left)
        def _():
            made[1].start()

    def land(made):
        @pl.when(has_left)
        def _():
            made[0].wait_recv()

        @pl.when(has_right)
        def _():
            made[1].wait_recv()

    def sent(made):
        @pl.when(has_right)
        def _():
            made[0].wait_send()

        @pl.when(has_left)
        def _():
            made[1].wait_send()

    @pl.when(me == 0)
    def _():
        src[:, 0:FH] = jnp.zeros((3, FH, ny, nz), F32)
        coef[0, 0:FH] = jnp.zeros((FH, ny, nz), F32)
        kcx[0 : CH + 1] = jnp.zeros((CH + 1, hy, hz), F32)
        csrc[:, 0:CH] = jnp.zeros((3, CH, hy, hz), F32)

    @pl.when(me == n - 1)
    def _():
        src[:, FH + cx : top] = jnp.zeros((3, FH, ny, nz), F32)
        coef[0, FH + cx : top] = jnp.zeros((FH, ny, nz), F32)
        kcx[CH + 1 + hx : ctop + 2] = jnp.zeros((CH + 1, hy, hz), F32)
        csrc[:, CH + hx : ctop] = jnp.zeros((3, CH, hy, hz), F32)

    def by_material(brick, values):
        m = mat[0, brick]
        return jnp.where(m == 0, values[0], jnp.where(m == 1, values[1], values[2]))

    get_mat.wait()
    get_stiff.wait()
    for brick in range(ny // BY):
        own = by_material(brick, MODULI)
        rows = slice(brick * BY, (brick + 1) * BY)
        coef[0, FH : FH + cx, rows] = raw[:, rows] * own

    get_force.wait()
    pl.semaphore_wait(barrier, n - 1 + loads - 1)
    start(coef_pair)
    start(near_pair)
    start(far_pair)

    rows_f = cx * ny
    zbits = nz.bit_length() - 1
    hbits = hz.bit_length() - 1
    get_src.wait()
    get_count.wait()
    get_dst.wait()

    @pl.loop(0, n)
    def _(owner):
        sub_z = lax.broadcasted_iota(jnp.int32, (nz, slots), 0)
        sub_r = lax.broadcasted_iota(jnp.int32, (rows_f, slots), 0)
        slot_r = lax.broadcasted_iota(jnp.int32, (rows_f, slots), 1)
        index = face_src[0, pl.ds(owner, 1), :]
        lanes = (sub_z == jnp.bitwise_and(index, nz - 1)).astype(F32).astype(BF16)
        lane_table[owner, 0:nz] = lanes
        lane_table[owner, nz : 2 * nz] = lanes
        live = jnp.logical_and(
            sub_r == lax.shift_right_logical(index, zbits), slot_r < count[0, owner]
        )
        live_table[owner] = live.astype(F32)
        sub_l = lax.broadcasted_iota(jnp.int32, (hz, slots), 0)
        index = face_dst[0, pl.ds(owner, 1), :]
        dst_table[owner] = (sub_l == jnp.bitwise_and(index, hz - 1)).astype(F32).astype(BF16)

    kview = coef.at[0]

    def diag_step(p):
        diag = fine.diag(kview, p)
        inside = jnp.logical_and(
            jnp.logical_or(p >= FH, has_left), jnp.logical_or(p < FH + cx, has_right)
        )
        keep = jnp.where(inside, 1.0, 0.0)
        coef[1, p] = diag + coef[0, p] * (1.0 / 7.0)
        coef[2, p] = keep / jnp.where(inside, diag, 1.0)

    factors = cheb_factors(FINE_STEPS)
    last = FH + cx
    planes_loop((FH + 1, last - 1, 2), diag_step)
    start_sweep((FH + 1, last - 1, 2), src, coef, d, va, wa)
    sweep(fine, (FH + 2, last - 2, 2), factors[0], src, coef, d, va, wa, vb, wb)
    sweep(fine, (FH + 3, last - 3, 2), factors[1], src, coef, d, vb, wb, va, wa)

    pool = (
        lax.shift_right_logical(lax.broadcasted_iota(jnp.int32, (nz, hz), 0), 1)
        == lax.broadcasted_iota(jnp.int32, (nz, hz), 1)
    ).astype(F32).astype(BF16)
    spread = (
        lax.shift_right_logical(lax.broadcasted_iota(jnp.int32, (hz, nz), 1), 1)
        == lax.broadcasted_iota(jnp.int32, (hz, nz), 0)
    ).astype(F32).astype(BF16)

    def pool_rows(i):
        return pooled[i, pl.ds(0, hy, stride=2), :] + pooled[i, pl.ds(1, hy, stride=2), :]

    def residual_step(p):
        image = fine.apply(va, wa, coef, p)
        for c in range(3):
            part = src[c, p] - image[c]
            res[c, p - FH] = part
            hi, lo = split(part)
            at = pl.ds(pl.multiple_of((p - FH) * ny, ny), ny)
            wide[c, at, 0:nz] = hi
            wide[c, at, nz : 2 * nz] = lo

    land(coef_pair)
    planes_loop([1, last - 1, FH], diag_step)

    count_c = hx + 2
    first = FH - 2
    stack = jnp.concatenate(
        [coef[0, first + 2 * i] + coef[0, first + 2 * i + 1] for i in range(count_c)], axis=0
    )
    pooled[0:count_c] = dot2(stack, pool).reshape(count_c, ny, hz)
    for i in range(count_c):
        kc[i] = pool_rows(i) * 0.125
    kcx[CH + 1 : CH + 1 + hx] = kc[1 : 1 + hx]

    land(near_pair)
    start_sweep([3, last - 1, 2], src, coef, d, va, wa)
    sweep(fine, [4, last - 2, 2], factors[0], src, coef, d, va, wa, vb, wb)
    sweep(fine, [5, last - 3, 2], factors[1], src, coef, d, vb, wb, va, wa)
    planes_loop([6, last - 4, 2], residual_step)
    land(far_pair)
    start_sweep([1, last + 1, 2], src, coef, d, va, wa)
    sweep(fine, [2, last, 2], factors[0], src, coef, d, va, wa, vb, wb)
    sweep(fine, [3, last - 1, 2], factors[1], src, coef, d, vb, wb, va, wa)
    planes_loop([4, last - 2, 2], residual_step)
    start(kc_pair)

    def pick(owner):
        live = live_table[owner]
        found = jnp.dot(
            wide[...].reshape(3 * rows_f, 2 * nz), lane_table[owner], preferred_element_type=F32
        )
        rows = [
            jnp.sum(found[c * rows_f : (c + 1) * rows_f] * live, axis=0, keepdims=True)
            for c in range(3)
        ]
        return jnp.concatenate(rows, axis=0)

    def a_copy(k):
        owner = lax.rem(me + k, n)
        return pltpu.make_async_remote_copy(
            src_ref=sendbuf.at[owner], dst_ref=arrived.at[me],
            send_sem=a_send.at[k], recv_sem=a_recv.at[k],
            device_id={"space": owner}, device_id_type=MESH,
        )

    group = 4 if n % 4 == 0 else 1

    @pl.loop(0, n // group)
    def _(i):
        ks = [i * group + 1 + j for j in range(group)]
        picked = [pick(lax.rem(me + k, n)) for k in ks]
        for k, values in zip(ks, picked):
            sendbuf[lax.rem(me + k, n)] = values
        for k in ks:

            @pl.when(k < n)
            def _(k=k):
                a_copy(k).start()

    arrived[me] = sendbuf[me]

    for c in range(3):
        stack = jnp.concatenate([res[c, 2 * i] + res[c, 2 * i + 1] for i in range(hx)], axis=0)
        pooled[0:hx] = dot2(stack, pool).reshape(hx, ny, hz)
        for i in range(hx):
            csrc[c, CH + i] = pool_rows(i) * 0.5

    rows_c = hx * hy
    sub_c = lax.broadcasted_iota(jnp.int32, (rows_c, slots), 0)

    def place(sender):
        index = face_dst[0, pl.ds(sender, 1), :]
        lanes = dst_table[sender]
        at_row = sub_c == lax.shift_right_logical(index, hbits)
        values = arrived[sender]
        parts = [jnp.where(at_row, values[c : c + 1], 0.0) for c in range(3)]
        hi, lo = split(jnp.concatenate(parts, axis=0))
        dims = (((1,), (1,)), ((), ()))
        return lax.dot_general(hi, lanes, dims, preferred_element_type=F32) + lax.dot_general(
            lo, lanes, dims, preferred_element_type=F32
        )

    total = place(me)

    @pl.loop(1, n)
    def _(k):
        a_copy(k).wait_recv()

    def add_sender(k, total):
        return total + place(lax.rem(me + n - k, n))

    total = lax.fori_loop(1, n, add_sender, total, unroll=min(n - 1, 7))
    csrc[:, CH : CH + hx] += total.reshape(3, hx, hy, hz)
    start(csrc_pair)
    land(kc_pair)
    for p in range(ctop):
        diag = coarse.diag(kcx, p + 1)
        k = kcx[p + 1]
        ccoef[0, p] = k
        ccoef[1, p] = diag + k * (1.0 / 7.0)
        if p < CH:
            keep = jnp.where(has_left, 1.0, 0.0)
            ccoef[2, p] = keep / jnp.where(has_left, diag, 1.0)
        elif p >= CH + hx:
            keep = jnp.where(has_right, 1.0, 0.0)
            ccoef[2, p] = keep / jnp.where(has_right, diag, 1.0)
        else:
            ccoef[2, p] = 1.0 / diag
    land(csrc_pair)

    factors = cheb_factors(COARSE_STEPS)
    start_sweep((0, ctop, ctop), csrc, ccoef, cd, cva, cwa)
    sweep(coarse, (1, ctop - 1, ctop - 2), factors[0], csrc, ccoef, cd, cva, cwa, cvb, cwb)
    sweep(coarse, (2, ctop - 2, ctop - 4), factors[1], csrc, ccoef, cd, cvb, cwb, cva, cwa)
    sweep(coarse, (3, ctop - 3, ctop - 6), factors[2], csrc, ccoef, cd, cva, cwa, cvb, cwb)

    fresh = hx + 2
    for c in range(3):
        lifted = dot2(cvb[c, 3 : 3 + fresh].reshape(fresh * hy, hz), spread)
        for i in range(fresh):
            plane = lifted[i * hy : (i + 1) * hy]
            for h in range(nz // 128):
                part = plane[:, h * 128 : (h + 1) * 128]
                lift[c, i, h, pl.ds(0, hy, stride=2), :] = part
                lift[c, i, h, pl.ds(1, hy, stride=2), :] = part
    for c in range(3):
        for i in range(fresh):
            doubled = jnp.concatenate([lift[c, i, h] for h in range(nz // 128)], axis=1)
            for p in (FH - 2 + 2 * i, FH - 1 + 2 * i):
                if FH - 1 <= p <= FH + cx:
                    moved = va[c, p] + doubled
                    vb[c, p] = moved
                    wb[c, p] = coef[0, p] * moved

    put_disp = pltpu.make_async_copy(
        vb.at[:, pl.ds(FH, cx)], disp_out.at[0], local_sem.at[2]
    )
    put_disp.start()

    part = ny // loads

    def energy_step(p):
        image = fine.apply(vb, wb, coef, p)
        energy = vb[0, p] * image[0] + vb[1, p] * image[1] + vb[2, p] * image[2]
        for i in range(loads):
            esend[i, p - FH] = energy[i * part : (i + 1) * part]

    halves = 2
    chunk = cx // halves

    def e_copy(k, half):
        owner = lax.rem(load + k, loads)
        return pltpu.make_async_remote_copy(
            src_ref=esend.at[owner, pl.ds(half * chunk, chunk)],
            dst_ref=erecv.at[k, pl.ds(half * chunk, chunk)],
            send_sem=e_send.at[k, half], recv_sem=e_recv.at[k, half],
            device_id={"load": owner}, device_id_type=MESH,
        )

    for half in range(halves):
        planes_loop((FH + half * chunk, FH + (half + 1) * chunk, 2), energy_step)
        for k in range(1, loads):
            e_copy(k, half).start()

    sent(near_pair)
    sent(far_pair)
    sent(coef_pair)
    sent(kc_pair)
    sent(csrc_pair)

    @pl.loop(1, n)
    def _(k):
        a_copy(k).wait_send()

    brick = (load * part) // BY
    ratios = [by_material(brick, [(modulus - own) / own for own in MODULI]) for modulus in MODULI]
    put_disp.wait()
    for half in range(halves):
        rows = slice(half * chunk, (half + 1) * chunk)
        total = esend[load, rows]
        for k in range(1, loads):
            e_copy(k, half).wait_recv()
            total = total + erecv[k, rows]
        for m in range(len(MODULI)):
            sens_out[m, rows] = total * ratios[m]
    for half in range(halves):
        for k in range(1, loads):
            e_copy(k, half).wait_send()


def deliver(disp, sens, disp_out, sens_out, disp_buf, sens_buf, sems):
    pieces = [(disp.at[0, c], disp_buf.at[c], disp_out.at[0, c]) for c in range(3)]
    pieces += [(sens.at[m], sens_buf.at[m], sens_out.at[m]) for m in range(3)]
    ins = [
        pltpu.make_async_copy(a, b, sems.at[0, i]) for i, (a, b, _) in enumerate(pieces)
    ]
    outs = [
        pltpu.make_async_copy(b, c, sems.at[1, i]) for i, (_, b, c) in enumerate(pieces)
    ]
    for copy in ins:
        copy.start()
    for arriving, leaving in zip(ins, outs):
        arriving.wait()
        leaving.start()
    for copy in outs:
        copy.wait()


def body(n, loads, load_force, stiffness, material, face_src, face_count, face_dst):
    cx, ny, nz = stiffness.shape
    hx, hy, hz = cx // 2, ny // 2, nz // 2
    slots = face_src.shape[2]
    part = ny // loads
    fine = (cx + 2 * FH, ny, nz)
    coarse = (hx + 2 * CH, hy, hz)
    vmem = pl.BlockSpec(memory_space=pltpu.VMEM)
    hbm = pl.BlockSpec(memory_space=pltpu.HBM)

    def buf(*shape):
        return pltpu.VMEM(shape, F32)

    dma = pltpu.SemaphoreType.DMA
    disp, sens = pl.pallas_call(
        functools.partial(kernel, n, loads),
        out_shape=(
            jax.ShapeDtypeStruct(load_force.shape, F32),
            jax.ShapeDtypeStruct((3, cx, part, nz), F32),
        ),
        in_specs=[hbm] * 6,
        out_specs=(hbm, vmem),
        scratch_shapes=[
            buf(3, *fine), buf(cx, ny, nz), buf(3, *fine), buf(3, *fine),
            buf(3, *fine), buf(3, *fine), buf(3, *fine), buf(3, *fine),
            buf(3, cx, ny, nz), buf(hx + 2, ny, hz), buf(hx + 2, hy, hz),
            buf(hx + 2 * CH + 2, hy, hz), buf(3, *coarse), buf(3, *coarse), buf(3, *coarse),
            buf(3, *coarse), buf(3, *coarse), buf(3, *coarse), buf(3, *coarse),
            buf(3, hx + 2, nz // 128, ny, 128),
            pltpu.SMEM(material.shape, jnp.int32), pltpu.VMEM(face_src.shape, jnp.int32),
            pltpu.SMEM(face_count.shape, jnp.int32), pltpu.VMEM(face_dst.shape, jnp.int32),
            pltpu.VMEM((n, 2 * nz, slots), BF16), buf(n, cx * ny, slots),
            pltpu.VMEM((n, hz, slots), BF16),
            pltpu.VMEM((3, cx * ny, 2 * nz), BF16),
            buf(n, 3, slots), buf(n, 3, slots),
            buf(loads, cx, part, nz), buf(loads, cx, part, nz),
            dma((7,)), dma((5, 2)), dma((5, 2)),
            dma((n,)), dma((n,)), dma((loads, 2)), dma((loads, 2)),
        ],
        compiler_params=pltpu.CompilerParams(
            collective_id=0, has_side_effects=True, vmem_limit_bytes=60 * 1024 * 1024
        ),
    )(load_force, stiffness, material, face_src, face_count, face_dst)
    return pl.pallas_call(
        deliver,
        out_shape=(
            jax.ShapeDtypeStruct(disp.shape, F32),
            jax.ShapeDtypeStruct(sens.shape, F32),
        ),
        in_specs=[hbm] * 2,
        out_specs=(hbm, hbm),
        scratch_shapes=[buf(*disp.shape[1:]), buf(*sens.shape), dma((2, 6))],
        compiler_params=pltpu.CompilerParams(vmem_limit_bytes=60 * 1024 * 1024),
    )(disp, sens)


def solution(mesh):
    return jax.shard_map(
        functools.partial(body, mesh.shape["space"], mesh.shape["load"]),
        mesh=mesh,
        in_specs=(
            P("load", None, "space", None, None),
            P("space", None, None),
            P("space", None),
            P("space", None, None),
            P("space", None),
            P("space", None, None),
        ),
        out_specs=(P("load", None, "space", None, None), P(None, "space", "load", None)),
        check_vma=False,
    )
```

```python
import functools

import jax
import jax.numpy as jnp
from jax import lax
from jax.experimental import pallas as pl
from jax.experimental.pallas import tpu as pltpu
from jax.sharding import PartitionSpec as P

BY = 8
FINE_STEPS = 3
COARSE_STEPS = 4
UPPER_EDGE = 2.1
LOWER_EDGE = 0.15
COUPLING = 0.1
MODULI = (1.0, 0.55, 0.25)

MID = (UPPER_EDGE + LOWER_EDGE) / 2.0
HALF = (UPPER_EDGE - LOWER_EDGE) / 2.0
F32 = jnp.float32
BF16 = jnp.bfloat16
MESH = pl.DeviceIdType.MESH
FH = 4
CH = 4


def cheb_factors(count):
    spread = MID / HALF
    rho = 1.0 / spread
    out = []
    for _ in range(1, count):
        rho_new = 1.0 / (2.0 * spread - rho)
        out.append((rho_new * rho, 2.0 * rho_new / HALF))
        rho = rho_new
    return out


def split(x):
    hi = x.astype(BF16)
    return hi, (x - hi.astype(F32)).astype(BF16)


def dot2(x, table):
    hi, lo = split(x)
    return jnp.dot(hi, table, preferred_element_type=F32) + jnp.dot(
        lo, table, preferred_element_type=F32
    )


class Plane:
    def __init__(self, rows, lanes):
        self.sizes = (rows, lanes)
        self.masks = []
        for axis, other in ((0, lanes), (1, rows)):
            shape = (8, other) if axis == 0 else (other, 128)
            place = lax.broadcasted_iota(jnp.int32, shape, axis)
            self.masks.append((place == shape[axis] - 1, place == 0))

    def shift(self, a, axis, up):
        tile = (8, 128)[axis]
        count = self.sizes[axis] // tile
        mask = self.masks[axis][0 if up else 1]
        turned = [
            pltpu.roll(
                lax.slice_in_dim(a, i * tile, (i + 1) * tile, axis=axis),
                tile - 1 if up else 1,
                axis,
            )
            for i in range(count)
        ]
        out = []
        for i in range(count):
            near = i + 1 if up else i - 1
            fill = turned[near] if 0 <= near < count else 0.0
            out.append(jnp.where(mask, fill, turned[i]))
        return out[0] if count == 1 else jnp.concatenate(out, axis=axis)

    def yp(self, a):
        return self.shift(a, 0, True)

    def ym(self, a):
        return self.shift(a, 0, False)

    def zp(self, a):
        return self.shift(a, 1, True)

    def zm(self, a):
        return self.shift(a, 1, False)

    def ty(self, a):
        return a + 0.5 * (self.yp(a) + self.ym(a))

    def tz(self, a):
        return a + 0.5 * (self.zp(a) + self.zm(a))

    def apply(self, v, w, coef, p):
        u0 = [v[c, p] for c in range(3)]
        um = [v[c, p - 1] for c in range(3)]
        up = [v[c, p + 1] for c in range(3)]
        a = [(u0[c] + 0.5 * (um[c] + up[c])) * (1.0 / 14.0) for c in range(3)]
        e = [(up[c] - um[c]) * (0.5 * COUPLING) for c in range(3)]
        b = [(w[c, p] + 0.5 * (w[c, p - 1] + w[c, p + 1])) * (1.0 / 14.0) for c in range(3)]
        half = 0.5 * COUPLING
        t = self.ty(a[0])
        mix_x = (
            t
            + 0.5 * (self.zp(t + e[2]) + self.zm(t - e[2]))
            + 0.5 * (self.yp(e[1]) - self.ym(e[1]))
        )
        t = self.tz(a[1])
        g = e[0] + half * (self.zp(u0[2]) - self.zm(u0[2]))
        mix_y = t + 0.5 * (self.yp(t + g) + self.ym(t - g))
        t = self.ty(a[2])
        g = e[0] + half * (self.yp(u0[1]) - self.ym(u0[1]))
        mix_z = t + 0.5 * (self.zp(t + g) + self.zm(t - g))
        k, dk = coef[0, p], coef[1, p]
        mix = (mix_x, mix_y, mix_z)
        return [dk * u0[c] - k * mix[c] - self.tz(self.ty(b[c])) for c in range(3)]

    def diag(self, k, p):
        t = k[p] + 0.5 * (k[p - 1] + k[p + 1])
        return (3.0 / 7.0) * k[p] + self.tz(self.ty(t)) * (1.0 / 14.0)


def planes_loop(planes, step):
    if isinstance(planes, list):
        low, other, count = planes

        def run(i, carry):
            step(low + i)
            step(other + i)
            return carry

        lax.fori_loop(0, count, run, 0)
        return
    low, high, unroll = planes

    def run(p, carry):
        step(p)
        return carry

    lax.fori_loop(low, high, run, 0, unroll=unroll)


def start_sweep(planes, src, coef, d, v, w):
    def step(p):
        scale = coef[2, p] * (1.0 / MID)
        k = coef[0, p]
        for c in range(3):
            new = src[c, p] * scale
            d[c, p] = new
            v[c, p] = new
            w[c, p] = k * new

    planes_loop(planes, step)


def sweep(plane, planes, factors, src, coef, d, v, w, v_out, w_out):
    alpha, beta = factors

    def step(p):
        image = plane.apply(v, w, coef, p)
        k = coef[0, p]
        scale = coef[2, p] * beta
        for c in range(3):
            new = alpha * d[c, p] + scale * (src[c, p] - image[c])
            d[c, p] = new
            total = v[c, p] + new
            v_out[c, p] = total
            w_out[c, p] = k * total

    planes_loop(planes, step)


def kernel(
    n, loads,
    force, stiff, mat_hbm, face_src_hbm, count_hbm, face_dst_hbm,
    disp_out, sens_out,
    src, raw, coef, d, va, wa, vb, wb, res, pooled, kc, kcx, ccoef, csrc, cd, cva, cwa, cvb, cwb,
    lift, mat, face_src, count, face_dst, lane_table, live_table, dst_table,
    wide, sendbuf, arrived, esend, erecv,
    local_sem, send_sem, recv_sem, a_send, a_recv, e_send, e_recv,
):
    me = lax.axis_index("space")
    load = lax.axis_index("load")
    cx, ny, nz = raw.shape
    hx, hy, hz = cx // 2, ny // 2, nz // 2
    fine = Plane(ny, nz)
    coarse = Plane(hy, hz)
    slots = face_src.shape[2]
    top = cx + 2 * FH
    ctop = hx + 2 * CH

    barrier = pltpu.get_barrier_semaphore()

    @pl.loop(1, n)
    def _(k):
        pl.semaphore_signal(
            barrier, inc=1, device_id={"space": lax.rem(me + k, n)}, device_id_type=MESH
        )

    @pl.loop(1, loads)
    def _(k):
        pl.semaphore_signal(
            barrier, inc=1, device_id={"load": lax.rem(load + k, loads)}, device_id_type=MESH
        )

    get_stiff = pltpu.make_async_copy(stiff, raw, local_sem.at[0])
    get_force = pltpu.make_async_copy(force.at[0], src.at[:, pl.ds(FH, cx)], local_sem.at[1])
    get_mat = pltpu.make_async_copy(mat_hbm, mat, local_sem.at[3])
    get_src = pltpu.make_async_copy(face_src_hbm, face_src, local_sem.at[4])
    get_count = pltpu.make_async_copy(count_hbm, count, local_sem.at[5])
    get_dst = pltpu.make_async_copy(face_dst_hbm, face_dst, local_sem.at[6])
    get_stiff.start()
    get_mat.start()
    get_force.start()
    get_src.start()
    get_count.start()
    get_dst.start()

    right = lax.rem(me + 1, n)
    left = lax.rem(me + n - 1, n)

    def pairs(base, ends):
        made = ([], [])
        for piece, ways in enumerate(ends):
            for side, ((at, to), target) in enumerate(zip(ways, (right, left))):
                made[side].append(
                    pltpu.make_async_remote_copy(
                        src_ref=at, dst_ref=to,
                        send_sem=send_sem.at[base + piece, side],
                        recv_sem=recv_sem.at[base + piece, side],
                        device_id={"space": target}, device_id_type=MESH,
                    )
                )
        return made

    far = FH - 2
    coef_pair = pairs(
        0,
        [
            (
                (coef.at[0, pl.ds(cx + i, 2)], coef.at[0, pl.ds(i, 2)]),
                (coef.at[0, pl.ds(FH + i, 2)], coef.at[0, pl.ds(FH + cx + i, 2)]),
            )
            for i in range(0, FH, 2)
        ],
    )
    near_pair = pairs(
        2,
        [
            (
                (src.at[c, pl.ds(FH + cx - 1, 1)], src.at[c, pl.ds(FH - 1, 1)]),
                (src.at[c, pl.ds(FH, 1)], src.at[c, pl.ds(FH + cx, 1)]),
            )
            for c in range(3)
        ],
    )
    far_pair = pairs(
        5,
        [
            (
                (src.at[c, pl.ds(FH + cx - 1 - far, far)], src.at[c, pl.ds(1, far)]),
                (src.at[c, pl.ds(FH + 1, far)], src.at[c, pl.ds(FH + cx + 1, far)]),
            )
            for c in range(3)
        ],
    )
    kc_pair = pairs(
        8,
        [
            (
                (kc.at[pl.ds(0, hx + 1)], kcx.at[pl.ds(0, hx + 1)]),
                (kc.at[pl.ds(1, hx + 1)], kcx.at[pl.ds(CH + 1 + hx, hx + 1)]),
            )
        ],
    )
    csrc_pair = pairs(
        9,
        [
            (
                (csrc.at[c, pl.ds(CH, hx)], csrc.at[c, pl.ds(0, hx)]),
                (csrc.at[c, pl.ds(CH, hx)], csrc.at[c, pl.ds(CH + hx, hx)]),
            )
            for c in range(3)
        ],
    )
    has_left, has_right = me > 0, me < n - 1

    def start(made):
        @pl.when(has_right)
        def _():
            for copy in made[0]:
                copy.start()

        @pl.when(has_left)
        def _():
            for copy in made[1]:
                copy.start()

    def land(made):
        @pl.when(has_left)
        def _():
            for copy in made[0]:
                copy.wait_recv()

        @pl.when(has_right)
        def _():
            for copy in made[1]:
                copy.wait_recv()

    def sent(made):
        @pl.when(has_right)
        def _():
            for copy in made[0]:
                copy.wait_send()

        @pl.when(has_left)
        def _():
            for copy in made[1]:
                copy.wait_send()

    @pl.when(me == 0)
    def _():
        src[:, 0:FH] = jnp.zeros((3, FH, ny, nz), F32)
        coef[0, 0:FH] = jnp.zeros((FH, ny, nz), F32)
        kcx[0 : CH + 1] = jnp.zeros((CH + 1, hy, hz), F32)
        csrc[:, 0:CH] = jnp.zeros((3, CH, hy, hz), F32)

    @pl.when(me == n - 1)
    def _():
        src[:, FH + cx : top] = jnp.zeros((3, FH, ny, nz), F32)
        coef[0, FH + cx : top] = jnp.zeros((FH, ny, nz), F32)
        kcx[CH + 1 + hx : ctop + 2] = jnp.zeros((CH + 1, hy, hz), F32)
        csrc[:, CH + hx : ctop] = jnp.zeros((3, CH, hy, hz), F32)

    def by_material(brick, values):
        m = mat[0, brick]
        return jnp.where(m == 0, values[0], jnp.where(m == 1, values[1], values[2]))

    get_mat.wait()
    get_stiff.wait()
    for brick in range(ny // BY):
        own = by_material(brick, MODULI)
        rows = slice(brick * BY, (brick + 1) * BY)
        coef[0, FH : FH + cx, rows] = raw[:, rows] * own

    get_force.wait()
    pl.semaphore_wait(barrier, n - 1 + loads - 1)
    start(coef_pair)
    start(near_pair)
    start(far_pair)

    rows_f = cx * ny
    zbits = nz.bit_length() - 1
    hbits = hz.bit_length() - 1
    get_src.wait()
    get_count.wait()
    get_dst.wait()

    @pl.loop(0, n)
    def _(owner):
        sub_z = lax.broadcasted_iota(jnp.int32, (nz, slots), 0)
        sub_r = lax.broadcasted_iota(jnp.int32, (rows_f, slots), 0)
        slot_r = lax.broadcasted_iota(jnp.int32, (rows_f, slots), 1)
        index = face_src[0, pl.ds(owner, 1), :]
        lanes = (sub_z == jnp.bitwise_and(index, nz - 1)).astype(F32).astype(BF16)
        lane_table[owner, 0:nz] = lanes
        lane_table[owner, nz : 2 * nz] = lanes
        live = jnp.logical_and(
            sub_r == lax.shift_right_logical(index, zbits), slot_r < count[0, owner]
        )
        live_table[owner] = live.astype(F32)
        sub_l = lax.broadcasted_iota(jnp.int32, (hz, slots), 0)
        index = face_dst[0, pl.ds(owner, 1), :]
        dst_table[owner] = (sub_l == jnp.bitwise_and(index, hz - 1)).astype(F32).astype(BF16)

    kview = coef.at[0]

    def diag_step(p):
        diag = fine.diag(kview, p)
        inside = jnp.logical_and(
            jnp.logical_or(p >= FH, has_left), jnp.logical_or(p < FH + cx, has_right)
        )
        keep = jnp.where(inside, 1.0, 0.0)
        coef[1, p] = diag + coef[0, p] * (1.0 / 7.0)
        coef[2, p] = keep / jnp.where(inside, diag, 1.0)

    factors = cheb_factors(FINE_STEPS)
    last = FH + cx
    planes_loop((FH + 1, last - 1, 2), diag_step)
    start_sweep((FH + 1, last - 1, 2), src, coef, d, va, wa)
    sweep(fine, (FH + 2, last - 2, 2), factors[0], src, coef, d, va, wa, vb, wb)
    sweep(fine, (FH + 3, last - 3, 2), factors[1], src, coef, d, vb, wb, va, wa)

    pool = (
        lax.shift_right_logical(lax.broadcasted_iota(jnp.int32, (nz, hz), 0), 1)
        == lax.broadcasted_iota(jnp.int32, (nz, hz), 1)
    ).astype(F32).astype(BF16)
    spread = (
        lax.shift_right_logical(lax.broadcasted_iota(jnp.int32, (hz, nz), 1), 1)
        == lax.broadcasted_iota(jnp.int32, (hz, nz), 0)
    ).astype(F32).astype(BF16)

    def pool_rows(i):
        return pooled[i, pl.ds(0, hy, stride=2), :] + pooled[i, pl.ds(1, hy, stride=2), :]

    def residual_step(p):
        image = fine.apply(va, wa, coef, p)
        for c in range(3):
            part = src[c, p] - image[c]
            res[c, p - FH] = part
            hi, lo = split(part)
            at = pl.ds(pl.multiple_of((p - FH) * ny, ny), ny)
            wide[c, at, 0:nz] = hi
            wide[c, at, nz : 2 * nz] = lo

    land(coef_pair)
    planes_loop([1, last - 1, FH], diag_step)

    count_c = hx + 2
    first = FH - 2
    stack = jnp.concatenate(
        [coef[0, first + 2 * i] + coef[0, first + 2 * i + 1] for i in range(count_c)], axis=0
    )
    pooled[0:count_c] = dot2(stack, pool).reshape(count_c, ny, hz)
    for i in range(count_c):
        kc[i] = pool_rows(i) * 0.125
    kcx[CH + 1 : CH + 1 + hx] = kc[1 : 1 + hx]

    land(near_pair)
    start_sweep([3, last - 1, 2], src, coef, d, va, wa)
    sweep(fine, [4, last - 2, 2], factors[0], src, coef, d, va, wa, vb, wb)
    sweep(fine, [5, last - 3, 2], factors[1], src, coef, d, vb, wb, va, wa)
    planes_loop([6, last - 4, 2], residual_step)
    land(far_pair)
    start_sweep([1, last + 1, 2], src, coef, d, va, wa)
    sweep(fine, [2, last, 2], factors[0], src, coef, d, va, wa, vb, wb)
    sweep(fine, [3, last - 1, 2], factors[1], src, coef, d, vb, wb, va, wa)
    planes_loop([4, last - 2, 2], residual_step)
    start(kc_pair)

    def pick(owner):
        live = live_table[owner]
        found = jnp.dot(
            wide[...].reshape(3 * rows_f, 2 * nz), lane_table[owner], preferred_element_type=F32
        )
        rows = [
            jnp.sum(found[c * rows_f : (c + 1) * rows_f] * live, axis=0, keepdims=True)
            for c in range(3)
        ]
        return jnp.concatenate(rows, axis=0)

    def a_copy(k):
        owner = lax.rem(me + k, n)
        return pltpu.make_async_remote_copy(
            src_ref=sendbuf.at[owner], dst_ref=arrived.at[me],
            send_sem=a_send.at[k], recv_sem=a_recv.at[k],
            device_id={"space": owner}, device_id_type=MESH,
        )

    group = 4 if n % 4 == 0 else 1

    @pl.loop(0, n // group)
    def _(i):
        ks = [i * group + 1 + j for j in range(group)]
        picked = [pick(lax.rem(me + k, n)) for k in ks]
        for k, values in zip(ks, picked):
            sendbuf[lax.rem(me + k, n)] = values
        for k in ks:

            @pl.when(k < n)
            def _(k=k):
                a_copy(k).start()

    arrived[me] = sendbuf[me]

    for c in range(3):
        stack = jnp.concatenate([res[c, 2 * i] + res[c, 2 * i + 1] for i in range(hx)], axis=0)
        pooled[0:hx] = dot2(stack, pool).reshape(hx, ny, hz)
        for i in range(hx):
            csrc[c, CH + i] = pool_rows(i) * 0.5

    rows_c = hx * hy
    sub_c = lax.broadcasted_iota(jnp.int32, (rows_c, slots), 0)

    def place(sender):
        index = face_dst[0, pl.ds(sender, 1), :]
        lanes = dst_table[sender]
        at_row = sub_c == lax.shift_right_logical(index, hbits)
        values = arrived[sender]
        parts = [jnp.where(at_row, values[c : c + 1], 0.0) for c in range(3)]
        hi, lo = split(jnp.concatenate(parts, axis=0))
        dims = (((1,), (1,)), ((), ()))
        return lax.dot_general(hi, lanes, dims, preferred_element_type=F32) + lax.dot_general(
            lo, lanes, dims, preferred_element_type=F32
        )

    total = place(me)

    @pl.loop(1, n)
    def _(k):
        a_copy(k).wait_recv()

    def add_sender(k, total):
        return total + place(lax.rem(me + n - k, n))

    total = lax.fori_loop(1, n, add_sender, total, unroll=min(n - 1, 7))
    csrc[:, CH : CH + hx] += total.reshape(3, hx, hy, hz)
    start(csrc_pair)
    land(kc_pair)
    for p in range(ctop):
        diag = coarse.diag(kcx, p + 1)
        k = kcx[p + 1]
        ccoef[0, p] = k
        ccoef[1, p] = diag + k * (1.0 / 7.0)
        if p < CH:
            keep = jnp.where(has_left, 1.0, 0.0)
            ccoef[2, p] = keep / jnp.where(has_left, diag, 1.0)
        elif p >= CH + hx:
            keep = jnp.where(has_right, 1.0, 0.0)
            ccoef[2, p] = keep / jnp.where(has_right, diag, 1.0)
        else:
            ccoef[2, p] = 1.0 / diag
    land(csrc_pair)

    factors = cheb_factors(COARSE_STEPS)
    start_sweep((0, ctop, ctop), csrc, ccoef, cd, cva, cwa)
    sweep(coarse, (1, ctop - 1, ctop - 2), factors[0], csrc, ccoef, cd, cva, cwa, cvb, cwb)
    sweep(coarse, (2, ctop - 2, ctop - 4), factors[1], csrc, ccoef, cd, cvb, cwb, cva, cwa)
    sweep(coarse, (3, ctop - 3, ctop - 6), factors[2], csrc, ccoef, cd, cva, cwa, cvb, cwb)

    fresh = hx + 2
    for c in range(3):
        lifted = dot2(cvb[c, 3 : 3 + fresh].reshape(fresh * hy, hz), spread)
        for i in range(fresh):
            plane = lifted[i * hy : (i + 1) * hy]
            for h in range(nz // 128):
                part = plane[:, h * 128 : (h + 1) * 128]
                lift[c, i, h, pl.ds(0, hy, stride=2), :] = part
                lift[c, i, h, pl.ds(1, hy, stride=2), :] = part
    for c in range(3):
        for i in range(fresh):
            doubled = jnp.concatenate([lift[c, i, h] for h in range(nz // 128)], axis=1)
            for p in (FH - 2 + 2 * i, FH - 1 + 2 * i):
                if FH - 1 <= p <= FH + cx:
                    moved = va[c, p] + doubled
                    vb[c, p] = moved
                    wb[c, p] = coef[0, p] * moved

    put_disp = pltpu.make_async_copy(
        vb.at[:, pl.ds(FH, cx)], disp_out.at[0], local_sem.at[2]
    )
    put_disp.start()

    part = ny // loads

    def energy_step(p):
        image = fine.apply(vb, wb, coef, p)
        energy = vb[0, p] * image[0] + vb[1, p] * image[1] + vb[2, p] * image[2]
        for i in range(loads):
            esend[i, p - FH] = energy[i * part : (i + 1) * part]

    halves = 2
    chunk = cx // halves

    def e_copy(k, half):
        owner = lax.rem(load + k, loads)
        return pltpu.make_async_remote_copy(
            src_ref=esend.at[owner, pl.ds(half * chunk, chunk)],
            dst_ref=erecv.at[k, pl.ds(half * chunk, chunk)],
            send_sem=e_send.at[k, half], recv_sem=e_recv.at[k, half],
            device_id={"load": owner}, device_id_type=MESH,
        )

    for half in range(halves):
        planes_loop((FH + half * chunk, FH + (half + 1) * chunk, 2), energy_step)
        for k in range(1, loads):
            e_copy(k, half).start()

    sent(near_pair)
    sent(far_pair)
    sent(coef_pair)
    sent(kc_pair)
    sent(csrc_pair)

    @pl.loop(1, n)
    def _(k):
        a_copy(k).wait_send()

    brick = (load * part) // BY
    ratios = [by_material(brick, [(modulus - own) / own for own in MODULI]) for modulus in MODULI]
    put_disp.wait()
    for half in range(halves):
        rows = slice(half * chunk, (half + 1) * chunk)
        total = esend[load, rows]
        for k in range(1, loads):
            e_copy(k, half).wait_recv()
            total = total + erecv[k, rows]
        for m in range(len(MODULI)):
            sens_out[m, rows] = total * ratios[m]
    for half in range(halves):
        for k in range(1, loads):
            e_copy(k, half).wait_send()


def deliver(disp, sens, disp_out, sens_out, disp_buf, sens_buf, sems):
    pieces = [(disp.at[0, c], disp_buf.at[c], disp_out.at[0, c]) for c in range(3)]
    pieces += [(sens.at[m], sens_buf.at[m], sens_out.at[m]) for m in range(3)]
    ins = [
        pltpu.make_async_copy(a, b, sems.at[0, i]) for i, (a, b, _) in enumerate(pieces)
    ]
    outs = [
        pltpu.make_async_copy(b, c, sems.at[1, i]) for i, (_, b, c) in enumerate(pieces)
    ]
    for copy in ins:
        copy.start()
    for arriving, leaving in zip(ins, outs):
        arriving.wait()
        leaving.start()
    for copy in outs:
        copy.wait()


def body(n, loads, load_force, stiffness, material, face_src, face_count, face_dst):
    cx, ny, nz = stiffness.shape
    hx, hy, hz = cx // 2, ny // 2, nz // 2
    slots = face_src.shape[2]
    part = ny // loads
    fine = (cx + 2 * FH, ny, nz)
    coarse = (hx + 2 * CH, hy, hz)
    vmem = pl.BlockSpec(memory_space=pltpu.VMEM)
    hbm = pl.BlockSpec(memory_space=pltpu.HBM)

    def buf(*shape):
        return pltpu.VMEM(shape, F32)

    dma = pltpu.SemaphoreType.DMA
    disp, sens = pl.pallas_call(
        functools.partial(kernel, n, loads),
        out_shape=(
            jax.ShapeDtypeStruct(load_force.shape, F32),
            jax.ShapeDtypeStruct((3, cx, part, nz), F32),
        ),
        in_specs=[hbm] * 6,
        out_specs=(hbm, vmem),
        scratch_shapes=[
            buf(3, *fine), buf(cx, ny, nz), buf(3, *fine), buf(3, *fine),
            buf(3, *fine), buf(3, *fine), buf(3, *fine), buf(3, *fine),
            buf(3, cx, ny, nz), buf(hx + 2, ny, hz), buf(hx + 2, hy, hz),
            buf(hx + 2 * CH + 2, hy, hz), buf(3, *coarse), buf(3, *coarse), buf(3, *coarse),
            buf(3, *coarse), buf(3, *coarse), buf(3, *coarse), buf(3, *coarse),
            buf(3, hx + 2, nz // 128, ny, 128),
            pltpu.SMEM(material.shape, jnp.int32), pltpu.VMEM(face_src.shape, jnp.int32),
            pltpu.SMEM(face_count.shape, jnp.int32), pltpu.VMEM(face_dst.shape, jnp.int32),
            pltpu.VMEM((n, 2 * nz, slots), BF16), buf(n, cx * ny, slots),
            pltpu.VMEM((n, hz, slots), BF16),
            pltpu.VMEM((3, cx * ny, 2 * nz), BF16),
            buf(n, 3, slots), buf(n, 3, slots),
            buf(loads, cx, part, nz), buf(loads, cx, part, nz),
            dma((7,)), dma((12, 2)), dma((12, 2)),
            dma((n,)), dma((n,)), dma((loads, 2)), dma((loads, 2)),
        ],
        compiler_params=pltpu.CompilerParams(
            collective_id=0, has_side_effects=True, vmem_limit_bytes=60 * 1024 * 1024
        ),
    )(load_force, stiffness, material, face_src, face_count, face_dst)
    return pl.pallas_call(
        deliver,
        out_shape=(
            jax.ShapeDtypeStruct(disp.shape, F32),
            jax.ShapeDtypeStruct(sens.shape, F32),
        ),
        in_specs=[hbm] * 2,
        out_specs=(hbm, hbm),
        scratch_shapes=[buf(*disp.shape[1:]), buf(*sens.shape), dma((2, 6))],
        compiler_params=pltpu.CompilerParams(vmem_limit_bytes=60 * 1024 * 1024),
    )(disp, sens)


def solution(mesh):
    return jax.shard_map(
        functools.partial(body, mesh.shape["space"], mesh.shape["load"]),
        mesh=mesh,
        in_specs=(
            P("load", None, "space", None, None),
            P("space", None, None),
            P("space", None),
            P("space", None, None),
            P("space", None),
            P("space", None, None),
        ),
        out_specs=(P("load", None, "space", None, None), P(None, "space", "load", None)),
        check_vma=False,
    )
```

```python
import functools

import jax
import jax.numpy as jnp
from jax import lax
from jax.experimental import pallas as pl
from jax.experimental.pallas import tpu as pltpu
from jax.sharding import PartitionSpec as P

BY = 8
FINE_STEPS = 3
COARSE_STEPS = 4
UPPER_EDGE = 2.1
LOWER_EDGE = 0.15
COUPLING = 0.1
MODULI = (1.0, 0.55, 0.25)

MID = (UPPER_EDGE + LOWER_EDGE) / 2.0
HALF = (UPPER_EDGE - LOWER_EDGE) / 2.0
F32 = jnp.float32
BF16 = jnp.bfloat16
MESH = pl.DeviceIdType.MESH
FH = 4
CH = 4


def cheb_factors(count):
    spread = MID / HALF
    rho = 1.0 / spread
    out = []
    for _ in range(1, count):
        rho_new = 1.0 / (2.0 * spread - rho)
        out.append((rho_new * rho, 2.0 * rho_new / HALF))
        rho = rho_new
    return out


def split(x):
    hi = x.astype(BF16)
    return hi, (x - hi.astype(F32)).astype(BF16)


def dot2(x, table):
    hi, lo = split(x)
    return jnp.dot(hi, table, preferred_element_type=F32) + jnp.dot(
        lo, table, preferred_element_type=F32
    )


class Plane:
    def __init__(self, rows, lanes):
        self.sizes = (rows, lanes)
        self.masks = []
        for axis, other in ((0, lanes), (1, rows)):
            shape = (8, other) if axis == 0 else (other, 128)
            place = lax.broadcasted_iota(jnp.int32, shape, axis)
            self.masks.append((place == shape[axis] - 1, place == 0))

    def shift(self, a, axis, up):
        tile = (8, 128)[axis]
        count = self.sizes[axis] // tile
        mask = self.masks[axis][0 if up else 1]
        turned = [
            pltpu.roll(
                lax.slice_in_dim(a, i * tile, (i + 1) * tile, axis=axis),
                tile - 1 if up else 1,
                axis,
            )
            for i in range(count)
        ]
        out = []
        for i in range(count):
            near = i + 1 if up else i - 1
            fill = turned[near] if 0 <= near < count else 0.0
            out.append(jnp.where(mask, fill, turned[i]))
        return out[0] if count == 1 else jnp.concatenate(out, axis=axis)

    def yp(self, a):
        return self.shift(a, 0, True)

    def ym(self, a):
        return self.shift(a, 0, False)

    def zp(self, a):
        return self.shift(a, 1, True)

    def zm(self, a):
        return self.shift(a, 1, False)

    def ty(self, a):
        return a + 0.5 * (self.yp(a) + self.ym(a))

    def tz(self, a):
        return a + 0.5 * (self.zp(a) + self.zm(a))

    def apply(self, v, w, coef, p):
        u0 = [v[c, p] for c in range(3)]
        um = [v[c, p - 1] for c in range(3)]
        up = [v[c, p + 1] for c in range(3)]
        a = [(u0[c] + 0.5 * (um[c] + up[c])) * (1.0 / 14.0) for c in range(3)]
        e = [(up[c] - um[c]) * (0.5 * COUPLING) for c in range(3)]
        b = [(w[c, p] + 0.5 * (w[c, p - 1] + w[c, p + 1])) * (1.0 / 14.0) for c in range(3)]
        half = 0.5 * COUPLING
        t = self.ty(a[0])
        mix_x = (
            t
            + 0.5 * (self.zp(t + e[2]) + self.zm(t - e[2]))
            + 0.5 * (self.yp(e[1]) - self.ym(e[1]))
        )
        t = self.tz(a[1])
        g = e[0] + half * (self.zp(u0[2]) - self.zm(u0[2]))
        mix_y = t + 0.5 * (self.yp(t + g) + self.ym(t - g))
        t = self.ty(a[2])
        g = e[0] + half * (self.yp(u0[1]) - self.ym(u0[1]))
        mix_z = t + 0.5 * (self.zp(t + g) + self.zm(t - g))
        k, dk = coef[0, p], coef[1, p]
        mix = (mix_x, mix_y, mix_z)
        return [dk * u0[c] - k * mix[c] - self.tz(self.ty(b[c])) for c in range(3)]

    def diag(self, k, p):
        t = k[p] + 0.5 * (k[p - 1] + k[p + 1])
        return (3.0 / 7.0) * k[p] + self.tz(self.ty(t)) * (1.0 / 14.0)


def planes_loop(planes, step):
    if isinstance(planes, list):
        low, other, count = planes

        def run(i, carry):
            step(low + i)
            step(other + i)
            return carry

        lax.fori_loop(0, count, run, 0)
        return
    low, high, unroll = planes

    def run(p, carry):
        step(p)
        return carry

    lax.fori_loop(low, high, run, 0, unroll=unroll)


def start_sweep(planes, src, coef, d, v, w):
    def step(p):
        scale = coef[2, p] * (1.0 / MID)
        k = coef[0, p]
        for c in range(3):
            new = src[c, p] * scale
            d[c, p] = new
            v[c, p] = new
            w[c, p] = k * new

    planes_loop(planes, step)


def sweep(plane, planes, factors, src, coef, d, v, w, v_out, w_out):
    alpha, beta = factors

    def step(p):
        image = plane.apply(v, w, coef, p)
        k = coef[0, p]
        scale = coef[2, p] * beta
        for c in range(3):
            new = alpha * d[c, p] + scale * (src[c, p] - image[c])
            d[c, p] = new
            total = v[c, p] + new
            v_out[c, p] = total
            w_out[c, p] = k * total

    planes_loop(planes, step)


def kernel(
    n, loads,
    force, stiff, mat_hbm, face_src_hbm, count_hbm, face_dst_hbm,
    disp_out, sens_out,
    src, raw, coef, d, va, wa, vb, wb, res, pooled, kc, kcx, ccoef, csrc, cd, cva, cwa, cvb, cwb,
    lift, mat, face_src, count, face_dst, lane_table, live_table, dst_table,
    wide, sendbuf, arrived, esend, erecv,
    local_sem, send_sem, recv_sem, a_send, a_recv, e_send, e_recv,
):
    me = lax.axis_index("space")
    load = lax.axis_index("load")
    cx, ny, nz = raw.shape
    hx, hy, hz = cx // 2, ny // 2, nz // 2
    fine = Plane(ny, nz)
    coarse = Plane(hy, hz)
    slots = face_src.shape[2]
    top = cx + 2 * FH
    ctop = hx + 2 * CH

    barrier = pltpu.get_barrier_semaphore()

    @pl.loop(1, n)
    def _(k):
        pl.semaphore_signal(
            barrier, inc=1, device_id={"space": lax.rem(me + k, n)}, device_id_type=MESH
        )

    @pl.loop(1, loads)
    def _(k):
        pl.semaphore_signal(
            barrier, inc=1, device_id={"load": lax.rem(load + k, loads)}, device_id_type=MESH
        )

    get_stiff = pltpu.make_async_copy(stiff, raw, local_sem.at[0])
    get_force = pltpu.make_async_copy(force.at[0], src.at[:, pl.ds(FH, cx)], local_sem.at[1])
    get_mat = pltpu.make_async_copy(mat_hbm, mat, local_sem.at[3])
    get_src = pltpu.make_async_copy(face_src_hbm, face_src, local_sem.at[4])
    get_count = pltpu.make_async_copy(count_hbm, count, local_sem.at[5])
    get_dst = pltpu.make_async_copy(face_dst_hbm, face_dst, local_sem.at[6])
    get_stiff.start()
    get_mat.start()
    get_force.start()
    get_src.start()
    get_count.start()
    get_dst.start()

    right = lax.rem(me + 1, n)
    left = lax.rem(me + n - 1, n)

    def pair(kind, to_right, to_left):
        made = []
        for side, (ends, target) in enumerate(((to_right, right), (to_left, left))):
            made.append(
                pltpu.make_async_remote_copy(
                    src_ref=ends[0], dst_ref=ends[1],
                    send_sem=send_sem.at[kind, side], recv_sem=recv_sem.at[kind, side],
                    device_id={"space": target}, device_id_type=MESH,
                )
            )
        return made

    far = FH - 2
    near_pair = pair(
        0,
        (src.at[:, pl.ds(FH + cx - 1, 1)], src.at[:, pl.ds(FH - 1, 1)]),
        (src.at[:, pl.ds(FH, 1)], src.at[:, pl.ds(FH + cx, 1)]),
    )
    far_pair = pair(
        4,
        (src.at[:, pl.ds(FH + cx - 1 - far, far)], src.at[:, pl.ds(1, far)]),
        (src.at[:, pl.ds(FH + 1, far)], src.at[:, pl.ds(FH + cx + 1, far)]),
    )
    coef_pair = pair(
        1,
        (coef.at[0, pl.ds(cx, FH)], coef.at[0, pl.ds(0, FH)]),
        (coef.at[0, pl.ds(FH, FH)], coef.at[0, pl.ds(FH + cx, FH)]),
    )
    kc_pair = pair(
        2,
        (kc.at[pl.ds(0, hx + 1)], kcx.at[pl.ds(0, hx + 1)]),
        (kc.at[pl.ds(1, hx + 1)], kcx.at[pl.ds(CH + 1 + hx, hx + 1)]),
    )
    csrc_pair = pair(
        3,
        (csrc.at[:, pl.ds(CH, hx)], csrc.at[:, pl.ds(0, hx)]),
        (csrc.at[:, pl.ds(CH, hx)], csrc.at[:, pl.ds(CH + hx, hx)]),
    )
    has_left, has_right = me > 0, me < n - 1

    def start(made):
        @pl.when(has_right)
        def _():
            made[0].start()

        @pl.when(has_left)
        def _():
            made[1].start()

    def land(made):
        @pl.when(has_left)
        def _():
            made[0].wait_recv()

        @pl.when(has_right)
        def _():
            made[1].wait_recv()

    def sent(made):
        @pl.when(has_right)
        def _():
            made[0].wait_send()

        @pl.when(has_left)
        def _():
            made[1].wait_send()

    @pl.when(me == 0)
    def _():
        src[:, 0:FH] = jnp.zeros((3, FH, ny, nz), F32)
        coef[0, 0:FH] = jnp.zeros((FH, ny, nz), F32)
        kcx[0 : CH + 1] = jnp.zeros((CH + 1, hy, hz), F32)
        csrc[:, 0:CH] = jnp.zeros((3, CH, hy, hz), F32)

    @pl.when(me == n - 1)
    def _():
        src[:, FH + cx : top] = jnp.zeros((3, FH, ny, nz), F32)
        coef[0, FH + cx : top] = jnp.zeros((FH, ny, nz), F32)
        kcx[CH + 1 + hx : ctop + 2] = jnp.zeros((CH + 1, hy, hz), F32)
        csrc[:, CH + hx : ctop] = jnp.zeros((3, CH, hy, hz), F32)

    def by_material(brick, values):
        m = mat[0, brick]
        return jnp.where(m == 0, values[0], jnp.where(m == 1, values[1], values[2]))

    get_mat.wait()
    get_stiff.wait()
    for brick in range(ny // BY):
        own = by_material(brick, MODULI)
        rows = slice(brick * BY, (brick + 1) * BY)
        coef[0, FH : FH + cx, rows] = raw[:, rows] * own

    get_force.wait()
    pl.semaphore_wait(barrier, n - 1 + loads - 1)
    start(coef_pair)
    start(near_pair)
    start(far_pair)

    rows_f = cx * ny
    zbits = nz.bit_length() - 1
    hbits = hz.bit_length() - 1
    get_src.wait()
    get_count.wait()
    get_dst.wait()

    @pl.loop(0, n)
    def _(owner):
        sub_z = lax.broadcasted_iota(jnp.int32, (nz, slots), 0)
        sub_r = lax.broadcasted_iota(jnp.int32, (rows_f, slots), 0)
        slot_r = lax.broadcasted_iota(jnp.int32, (rows_f, slots), 1)
        index = face_src[0, pl.ds(owner, 1), :]
        lanes = (sub_z == jnp.bitwise_and(index, nz - 1)).astype(F32).astype(BF16)
        lane_table[owner, 0:nz] = lanes
        lane_table[owner, nz : 2 * nz] = lanes
        live = jnp.logical_and(
            sub_r == lax.shift_right_logical(index, zbits), slot_r < count[0, owner]
        )
        live_table[owner] = live.astype(F32)
        sub_l = lax.broadcasted_iota(jnp.int32, (hz, slots), 0)
        index = face_dst[0, pl.ds(owner, 1), :]
        dst_table[owner] = (sub_l == jnp.bitwise_and(index, hz - 1)).astype(F32).astype(BF16)

    kview = coef.at[0]

    def diag_step(p):
        diag = fine.diag(kview, p)
        inside = jnp.logical_and(
            jnp.logical_or(p >= FH, has_left), jnp.logical_or(p < FH + cx, has_right)
        )
        keep = jnp.where(inside, 1.0, 0.0)
        coef[1, p] = diag + coef[0, p] * (1.0 / 7.0)
        coef[2, p] = keep / jnp.where(inside, diag, 1.0)

    factors = cheb_factors(FINE_STEPS)
    last = FH + cx
    planes_loop((FH + 1, last - 1, 2), diag_step)
    start_sweep((FH + 1, last - 1, 2), src, coef, d, va, wa)
    sweep(fine, (FH + 2, last - 2, 2), factors[0], src, coef, d, va, wa, vb, wb)
    sweep(fine, (FH + 3, last - 3, 2), factors[1], src, coef, d, vb, wb, va, wa)

    pool = (
        lax.shift_right_logical(lax.broadcasted_iota(jnp.int32, (nz, hz), 0), 1)
        == lax.broadcasted_iota(jnp.int32, (nz, hz), 1)
    ).astype(F32).astype(BF16)
    spread = (
        lax.shift_right_logical(lax.broadcasted_iota(jnp.int32, (hz, nz), 1), 1)
        == lax.broadcasted_iota(jnp.int32, (hz, nz), 0)
    ).astype(F32).astype(BF16)

    def pool_rows(i):
        return pooled[i, pl.ds(0, hy, stride=2), :] + pooled[i, pl.ds(1, hy, stride=2), :]

    def residual_step(p):
        image = fine.apply(va, wa, coef, p)
        for c in range(3):
            part = src[c, p] - image[c]
            res[c, p - FH] = part
            hi, lo = split(part)
            at = pl.ds(pl.multiple_of((p - FH) * ny, ny), ny)
            wide[c, at, 0:nz] = hi
            wide[c, at, nz : 2 * nz] = lo

    land(coef_pair)
    planes_loop([1, last - 1, FH], diag_step)

    count_c = hx + 2
    first = FH - 2
    stack = jnp.concatenate(
        [coef[0, first + 2 * i] + coef[0, first + 2 * i + 1] for i in range(count_c)], axis=0
    )
    pooled[0:count_c] = dot2(stack, pool).reshape(count_c, ny, hz)
    for i in range(count_c):
        kc[i] = pool_rows(i) * 0.125
    kcx[CH + 1 : CH + 1 + hx] = kc[1 : 1 + hx]

    land(near_pair)
    start_sweep([3, last - 1, 2], src, coef, d, va, wa)
    sweep(fine, [4, last - 2, 2], factors[0], src, coef, d, va, wa, vb, wb)
    sweep(fine, [5, last - 3, 2], factors[1], src, coef, d, vb, wb, va, wa)
    planes_loop([6, last - 4, 2], residual_step)
    land(far_pair)
    start_sweep([1, last + 1, 2], src, coef, d, va, wa)
    sweep(fine, [2, last, 2], factors[0], src, coef, d, va, wa, vb, wb)
    sweep(fine, [3, last - 1, 2], factors[1], src, coef, d, vb, wb, va, wa)
    planes_loop([4, last - 2, 2], residual_step)
    start(kc_pair)

    def pick(owner):
        live = live_table[owner]
        found = jnp.dot(
            wide[...].reshape(3 * rows_f, 2 * nz), lane_table[owner], preferred_element_type=F32
        )
        rows = [
            jnp.sum(found[c * rows_f : (c + 1) * rows_f] * live, axis=0, keepdims=True)
            for c in range(3)
        ]
        return jnp.concatenate(rows, axis=0)

    def a_copy(k):
        owner = lax.rem(me + k, n)
        return pltpu.make_async_remote_copy(
            src_ref=sendbuf.at[owner], dst_ref=arrived.at[me],
            send_sem=a_send.at[k], recv_sem=a_recv.at[k],
            device_id={"space": owner}, device_id_type=MESH,
        )

    group = 4 if n % 4 == 0 else 1

    @pl.loop(0, n // group)
    def _(i):
        ks = [i * group + 1 + j for j in range(group)]
        picked = [pick(lax.rem(me + k, n)) for k in ks]
        for k, values in zip(ks, picked):
            sendbuf[lax.rem(me + k, n)] = values
        for k in ks:

            @pl.when(k < n)
            def _(k=k):
                a_copy(k).start()

    arrived[me] = sendbuf[me]

    for c in range(3):
        stack = jnp.concatenate([res[c, 2 * i] + res[c, 2 * i + 1] for i in range(hx)], axis=0)
        pooled[0:hx] = dot2(stack, pool).reshape(hx, ny, hz)
        for i in range(hx):
            csrc[c, CH + i] = pool_rows(i) * 0.5

    rows_c = hx * hy
    sub_c = lax.broadcasted_iota(jnp.int32, (rows_c, slots), 0)

    def place(sender):
        index = face_dst[0, pl.ds(sender, 1), :]
        lanes = dst_table[sender]
        at_row = sub_c == lax.shift_right_logical(index, hbits)
        values = arrived[sender]
        parts = [jnp.where(at_row, values[c : c + 1], 0.0) for c in range(3)]
        hi, lo = split(jnp.concatenate(parts, axis=0))
        dims = (((1,), (1,)), ((), ()))
        return lax.dot_general(hi, lanes, dims, preferred_element_type=F32) + lax.dot_general(
            lo, lanes, dims, preferred_element_type=F32
        )

    total = place(me)

    @pl.loop(1, n)
    def _(k):
        a_copy(k).wait_recv()

    def add_sender(k, total):
        return total + place(lax.rem(me + n - k, n))

    total = lax.fori_loop(1, n, add_sender, total, unroll=min(n - 1, 7))
    csrc[:, CH : CH + hx] += total.reshape(3, hx, hy, hz)
    start(csrc_pair)
    land(kc_pair)
    for p in range(ctop):
        diag = coarse.diag(kcx, p + 1)
        k = kcx[p + 1]
        ccoef[0, p] = k
        ccoef[1, p] = diag + k * (1.0 / 7.0)
        if p < CH:
            keep = jnp.where(has_left, 1.0, 0.0)
            ccoef[2, p] = keep / jnp.where(has_left, diag, 1.0)
        elif p >= CH + hx:
            keep = jnp.where(has_right, 1.0, 0.0)
            ccoef[2, p] = keep / jnp.where(has_right, diag, 1.0)
        else:
            ccoef[2, p] = 1.0 / diag
    land(csrc_pair)

    factors = cheb_factors(COARSE_STEPS)
    start_sweep((0, ctop, ctop), csrc, ccoef, cd, cva, cwa)
    sweep(coarse, (1, ctop - 1, ctop - 2), factors[0], csrc, ccoef, cd, cva, cwa, cvb, cwb)
    sweep(coarse, (2, ctop - 2, ctop - 4), factors[1], csrc, ccoef, cd, cvb, cwb, cva, cwa)
    sweep(coarse, (3, ctop - 3, ctop - 6), factors[2], csrc, ccoef, cd, cva, cwa, cvb, cwb)

    fresh = hx + 2
    for c in range(3):
        lifted = dot2(cvb[c, 3 : 3 + fresh].reshape(fresh * hy, hz), spread)
        for i in range(fresh):
            plane = lifted[i * hy : (i + 1) * hy]
            for h in range(nz // 128):
                part = plane[:, h * 128 : (h + 1) * 128]
                lift[c, i, h, pl.ds(0, hy, stride=2), :] = part
                lift[c, i, h, pl.ds(1, hy, stride=2), :] = part
    for c in range(3):
        for i in range(fresh):
            doubled = jnp.concatenate([lift[c, i, h] for h in range(nz // 128)], axis=1)
            for p in (FH - 2 + 2 * i, FH - 1 + 2 * i):
                if FH - 1 <= p <= FH + cx:
                    moved = va[c, p] + doubled
                    vb[c, p] = moved
                    if FH <= p < FH + cx:
                        disp_out[0, c, p - FH] = moved
                    wb[c, p] = coef[0, p] * moved

    part = ny // loads

    def energy_step(p):
        image = fine.apply(vb, wb, coef, p)
        energy = vb[0, p] * image[0] + vb[1, p] * image[1] + vb[2, p] * image[2]
        for i in range(loads):
            esend[i, p - FH] = energy[i * part : (i + 1) * part]

    halves = 2
    chunk = cx // halves

    def e_copy(k, half):
        owner = lax.rem(load + k, loads)
        return pltpu.make_async_remote_copy(
            src_ref=esend.at[owner, pl.ds(half * chunk, chunk)],
            dst_ref=erecv.at[k, pl.ds(half * chunk, chunk)],
            send_sem=e_send.at[k, half], recv_sem=e_recv.at[k, half],
            device_id={"load": owner}, device_id_type=MESH,
        )

    for half in range(halves):
        planes_loop((FH + half * chunk, FH + (half + 1) * chunk, 2), energy_step)
        for k in range(1, loads):
            e_copy(k, half).start()

    sent(near_pair)
    sent(far_pair)
    sent(coef_pair)
    sent(kc_pair)
    sent(csrc_pair)

    @pl.loop(1, n)
    def _(k):
        a_copy(k).wait_send()

    brick = (load * part) // BY
    ratios = [by_material(brick, [(modulus - own) / own for own in MODULI]) for modulus in MODULI]
    for half in range(halves):
        rows = slice(half * chunk, (half + 1) * chunk)
        total = esend[load, rows]
        for k in range(1, loads):
            e_copy(k, half).wait_recv()
            total = total + erecv[k, rows]
        for m in range(len(MODULI)):
            sens_out[m, rows] = total * ratios[m]
    for half in range(halves):
        for k in range(1, loads):
            e_copy(k, half).wait_send()


def deliver(disp, sens, disp_out, sens_out, sems):
    copies = [
        pltpu.make_async_copy(disp.at[0, c], disp_out.at[0, c], sems.at[c]) for c in range(3)
    ]
    copies.append(pltpu.make_async_copy(sens, sens_out, sems.at[3]))
    for copy in copies:
        copy.start()
    for copy in copies:
        copy.wait()


def body(n, loads, load_force, stiffness, material, face_src, face_count, face_dst):
    cx, ny, nz = stiffness.shape
    hx, hy, hz = cx // 2, ny // 2, nz // 2
    slots = face_src.shape[2]
    part = ny // loads
    fine = (cx + 2 * FH, ny, nz)
    coarse = (hx + 2 * CH, hy, hz)
    vmem = pl.BlockSpec(memory_space=pltpu.VMEM)
    hbm = pl.BlockSpec(memory_space=pltpu.HBM)

    def buf(*shape):
        return pltpu.VMEM(shape, F32)

    dma = pltpu.SemaphoreType.DMA
    disp, sens = pl.pallas_call(
        functools.partial(kernel, n, loads),
        out_shape=(
            pltpu.VMEM(load_force.shape, F32),
            pltpu.VMEM((3, cx, part, nz), F32),
        ),
        in_specs=[hbm] * 6,
        out_specs=(vmem, vmem),
        scratch_shapes=[
            buf(3, *fine), buf(cx, ny, nz), buf(3, *fine), buf(3, *fine),
            buf(3, *fine), buf(3, *fine), buf(3, *fine), buf(3, *fine),
            buf(3, cx, ny, nz), buf(hx + 2, ny, hz), buf(hx + 2, hy, hz),
            buf(hx + 2 * CH + 2, hy, hz), buf(3, *coarse), buf(3, *coarse), buf(3, *coarse),
            buf(3, *coarse), buf(3, *coarse), buf(3, *coarse), buf(3, *coarse),
            buf(3, hx + 2, nz // 128, ny, 128),
            pltpu.SMEM(material.shape, jnp.int32), pltpu.VMEM(face_src.shape, jnp.int32),
            pltpu.SMEM(face_count.shape, jnp.int32), pltpu.VMEM(face_dst.shape, jnp.int32),
            pltpu.VMEM((n, 2 * nz, slots), BF16), buf(n, cx * ny, slots),
            pltpu.VMEM((n, hz, slots), BF16),
            pltpu.VMEM((3, cx * ny, 2 * nz), BF16),
            buf(n, 3, slots), buf(n, 3, slots),
            buf(loads, cx, part, nz), buf(loads, cx, part, nz),
            dma((7,)), dma((5, 2)), dma((5, 2)),
            dma((n,)), dma((n,)), dma((loads, 2)), dma((loads, 2)),
        ],
        compiler_params=pltpu.CompilerParams(
            collective_id=0, has_side_effects=True, vmem_limit_bytes=60 * 1024 * 1024
        ),
    )(load_force, stiffness, material, face_src, face_count, face_dst)
    return pl.pallas_call(
        deliver,
        out_shape=(
            jax.ShapeDtypeStruct(disp.shape, F32),
            jax.ShapeDtypeStruct(sens.shape, F32),
        ),
        in_specs=[vmem] * 2,
        out_specs=(hbm, hbm),
        scratch_shapes=[dma((4,))],
        compiler_params=pltpu.CompilerParams(vmem_limit_bytes=4 * 1024 * 1024),
    )(disp, sens)


def solution(mesh):
    return jax.shard_map(
        functools.partial(body, mesh.shape["space"], mesh.shape["load"]),
        mesh=mesh,
        in_specs=(
            P("load", None, "space", None, None),
            P("space", None, None),
            P("space", None),
            P("space", None, None),
            P("space", None),
            P("space", None, None),
        ),
        out_specs=(P("load", None, "space", None, None), P(None, "space", "load", None)),
        check_vma=False,
    )
```
